32 devices in a mesh: slab: 8 (over z, x), tile: 4 (over y, core).
Axes of the slice: x: 2, y: 2, z: 4, core: 2. Of those that a mesh axis runs over, the one named last changes fastest.
Arguments:
- encoded: bfloat16 [8, 16, 2048, 128], P('slab', None, 'tile'), may hold values from -6 to 6
- spacing: float32 [8, 16, 2048], P('slab', None, 'tile'), may hold values from 0.002 to 0.05
- counts: int32 [8, 2048], P('slab', 'tile'), may hold values from 1 to 16
- seg_first: int32 [2048], P('tile'), may hold values from 0 to 1
- seg_last: int32 [2048], P('tile'), may hold values from 7 to 8
- direction: int32 [2048], P('tile'), may hold values from 0 to 1
- field_in: bfloat16 [8, 128, 256], P('slab'), may hold values from -0.5 to 0.5
- field_mid: bfloat16 [8, 256, 256], P('slab'), may hold values from -0.375 to 0.375
- field_out: bfloat16 [8, 256, 64], P('slab'), may hold values from -0.375 to 0.375
- color_head: float32 [64, 3], replicated, may hold values from -0.75 to 0.75
- target: float32 [2048, 3], P('tile'), may hold values from 0 to 1
Outputs:
- front_trans: float32 [8, 2048], P('slab', 'tile')
- grad_in: float32 [8, 128, 256], P('slab')
- grad_mid: float32 [8, 256, 256], P('slab')
- grad_out: float32 [8, 256, 64], P('slab')
The draws below stay inside these ranges and needn't reach their ends.
All inputs are finite; a program needn't handle non-finite values.
Results may differ from the reference program's by a relative error of at most 0.014.
The reference program's roundings to bfloat16 on the way (of `hidden_one`, `hidden_two`, `grad_low`, `back_two` and `back_one`) count: a program that leaves them out, or rounds other values in their place, can miss the bound.
Values sent between devices are 32-bit elements; how exact they have to be, the bound alone decides.
No kernel may reach another device: no remote copies, remote signals or barrier semaphores. Data moves between devices by JAX's collectives and lax.ppermute only.
A program may use at most 64 MiB of HBM per device.

```python
import math
import jax
import jax.numpy as jnp
from jax import lax

ENC = 128
HID = 256
OUT = 64
SAMP = 16
RAYS_DEV = 512
SLABS = 8
RAYS = 2048
N_SLAB = 8


def set_ends(values, stream_key, smallest, top_value):
    longest = values.shape.index(max(values.shape))
    spots = []
    for shift in (0, 1):
        where = [jax.random.randint(jax.random.fold_in(stream_key, axis), (), 0, length) for axis, length in enumerate(values.shape)]
        where[longest] = (where[longest] + shift) % values.shape[longest]
        spots.append(tuple(where))
    return values.at[spots[0]].set(smallest).at[spots[1]].set(top_value)


def block_levels(stream_key, extent, pieces, least, top_value):
    level, own = 1.0, jax.random.fold_in(stream_key, 6)
    for dim, blocks in pieces:
        heights = jnp.exp(jax.random.uniform(jax.random.fold_in(own, dim), (blocks,), jnp.float32, least / len(pieces), top_value / len(pieces)))
        level = level * jnp.repeat(heights, extent[dim] // blocks).reshape([-1 if axis == dim else 1 for axis in range(len(extent))])
    return level


def centred(stream_key, shape, scale, reach, split=(), kind=jnp.bfloat16):
    factor_of = block_levels(stream_key, shape, split, -0.22, 0.18) if split else 1.0
    drawn = jax.random.normal(stream_key, shape, jnp.float32) * scale * factor_of
    return jnp.minimum(jnp.maximum(drawn, -reach), reach).astype(kind)


def setup_inputs(seed: int = 0) -> dict:
    key_list = jax.random.split(jax.random.key(seed), 12)
    return {
        "encoded": centred(key_list[0], (SLABS, SAMP, RAYS, ENC), 1.0, 6.0, ((0, 8), (2, 4))),
        "spacing": jnp.clip(jnp.exp(math.log(0.05) - 3.218876 * jax.random.uniform(key_list[1], (SLABS, SAMP, RAYS), jnp.float32) ** block_levels(key_list[1], (SLABS, SAMP, RAYS), ((0, 8), (2, 4)), -0.2, 0.2)), 0.002, 0.05),
        "counts": set_ends(jax.random.randint(key_list[2], (SLABS, RAYS), 1, SAMP + 1), jax.random.fold_in(key_list[2], 1), 1, SAMP).astype(jnp.int32),
        "seg_first": set_ends(jax.random.randint(key_list[3], (RAYS,), 0, N_SLAB // 4), jax.random.fold_in(key_list[3], 1), 0, (N_SLAB // 4) - 1).astype(jnp.int32),
        "seg_last": set_ends(jax.random.randint(key_list[4], (RAYS,), N_SLAB - N_SLAB // 4 + 1, N_SLAB + 1), jax.random.fold_in(key_list[4], 1), N_SLAB - N_SLAB // 4 + 1, N_SLAB).astype(jnp.int32),
        "direction": set_ends(jax.random.randint(key_list[5], (RAYS,), 0, 2), jax.random.fold_in(key_list[5], 1), 0, 1).astype(jnp.int32),
        "field_in": centred(key_list[6], (SLABS, ENC, HID), ENC ** -0.5, 0.5, ((0, 8),)),
        "field_mid": centred(key_list[7], (SLABS, HID, HID), HID ** -0.5, 0.375, ((0, 8),)),
        "field_out": centred(key_list[8], (SLABS, HID, OUT), HID ** -0.5, 0.375, ((0, 8),)),
        "color_head": centred(key_list[9], (OUT, 3), OUT ** -0.5, 0.75, (), jnp.float32),
        "target": jnp.clip(1.0 * jax.random.uniform(key_list[10], (RAYS, 3), jnp.float32) ** block_levels(key_list[10], (RAYS, 3), ((0, 4),), -0.2, 0.2), 0.0, 1.0),
    }


def field(field_in, field_mid, field_out, inputs):
    hidden_one = jax.nn.relu(jnp.dot(inputs, field_in, preferred_element_type=jnp.float32)).astype(jnp.bfloat16)
    hidden_two = jax.nn.relu(jnp.dot(hidden_one, field_mid, preferred_element_type=jnp.float32)).astype(jnp.bfloat16)
    outputs = jnp.dot(hidden_two, field_out, preferred_element_type=jnp.float32)
    return (hidden_one, hidden_two, outputs)

def composite(outputs, spacing, live_mask, direction):
    optical = jax.nn.softplus(outputs[:, :, 0]) * spacing * live_mask
    running = jnp.cumsum(optical, axis=0)
    column_sum = running[-1]
    before = jnp.where(direction[None, :] > 0, column_sum[None, :] - running, running - optical)
    weights = jnp.exp(-before) * (1.0 - jnp.exp(-optical))
    colors = lax.optimization_barrier(jnp.sum(weights[:, :, None] * outputs, axis=0))
    return (jnp.exp(-column_sum), colors)

def make_combine(front_first):

    def combine(earlier, later):
        trans_early, color_early = earlier
        trans_late, color_late = later
        joined = jnp.where(front_first[:, None], color_early + trans_early[:, None] * color_late, color_late + trans_late[:, None] * color_early)
        return (trans_early * trans_late, joined)
    return combine

def field_grads(field_mid, field_out, inputs, hidden_one, hidden_two, grad_outputs):
    grad_low = grad_outputs.astype(jnp.bfloat16)
    grad_three = jnp.dot(hidden_two.T, grad_low, preferred_element_type=jnp.float32)
    back_two = (jnp.dot(grad_low, field_out.T, preferred_element_type=jnp.float32) * (hidden_two > 0)).astype(jnp.bfloat16)
    grad_two = jnp.dot(hidden_one.T, back_two, preferred_element_type=jnp.float32)
    back_one = (jnp.dot(back_two, field_mid.T, preferred_element_type=jnp.float32) * (hidden_one > 0)).astype(jnp.bfloat16)
    grad_one = jnp.dot(inputs.T, back_one, preferred_element_type=jnp.float32)
    return (grad_one, grad_two, grad_three)

def pixel_grad(color_total, color_head, target):
    logits = jnp.dot(color_total, color_head, precision=lax.Precision.HIGHEST)
    shade = jax.nn.sigmoid(logits)
    error = (shade - target) / RAYS_DEV
    return jnp.dot(error * shade * (1.0 - shade), color_head.T, precision=lax.Precision.HIGHEST)

def reference(encoded, spacing, counts, seg_first, seg_last, direction, field_in, field_mid, field_out, color_head, target):
    slab_ids = jnp.arange(N_SLAB, dtype=jnp.int32)
    sample_ids = jnp.arange(SAMP, dtype=jnp.int32)
    reverse_rays = direction > 0

    def live_of(slab):
        active = (seg_first <= slab) & (slab < seg_last)
        return ((sample_ids[:, None] < counts[slab][None, :]) & active[None, :]).astype(jnp.float32)

    def forward(slab):
        inputs = encoded[slab].reshape(-1, ENC)
        _, _, outputs = field(field_in[slab], field_mid[slab], field_out[slab], inputs)
        return composite(outputs.reshape(SAMP, -1, OUT), spacing[slab], live_of(slab), direction)
    seg_trans, seg_color = lax.map(forward, slab_ids)
    combine_low = make_combine(jnp.logical_not(reverse_rays))
    combine_high = make_combine(reverse_rays)
    identity = (jnp.ones((RAYS,), jnp.float32), jnp.zeros((RAYS, OUT), jnp.float32))

    def step_low(running_pair, item):
        return (combine_low(running_pair, item), running_pair)

    def step_high(running_pair, item):
        return (combine_high(running_pair, item), running_pair)
    final_pair, low_pairs = lax.scan(step_low, identity, (seg_trans, seg_color))
    _, high_pairs = lax.scan(step_high, identity, (seg_trans, seg_color), reverse=True)
    grad_color = pixel_grad(final_pair[1], color_head, target)
    front_trans = jnp.where(reverse_rays[None, :], high_pairs[0], low_pairs[0])
    back_color = jnp.where(reverse_rays[None, :, None], low_pairs[1], high_pairs[1])

    def backward(slab):
        inputs = encoded[slab].reshape(-1, ENC)
        hidden_one, hidden_two, outputs = field(field_in[slab], field_mid[slab], field_out[slab], inputs)
        live_mask = live_of(slab)
        space_here = spacing[slab]
        front_here = front_trans[slab]
        grad_seg_color = front_here[:, None] * grad_color
        grad_seg_trans = front_here * lax.optimization_barrier(jnp.sum(grad_color * back_color[slab], axis=1))
        _, pull_back = jax.vjp(lambda values: composite(values, space_here, live_mask, direction), outputs.reshape(SAMP, -1, OUT))
        grad_outputs = pull_back((grad_seg_trans, grad_seg_color))[0].reshape(-1, OUT)
        return field_grads(field_mid[slab], field_out[slab], inputs, hidden_one, hidden_two, grad_outputs)
    grad_in, grad_mid, grad_out = lax.map(backward, slab_ids)
    return (front_trans, grad_in, grad_mid, grad_out)
```

```python
import functools

import jax
import jax.numpy as jnp
from jax import lax
from jax.experimental import pallas as pl
from jax.experimental.pallas import tpu as pltpu
from jax.sharding import PartitionSpec as P

F32 = jnp.float32
BF16 = jnp.bfloat16
VMEM = pl.BlockSpec(memory_space=pltpu.VMEM)
SMEM = pl.BlockSpec(memory_space=pltpu.SMEM)
ANY = pl.BlockSpec(memory_space=pl.ANY)
LIMIT = pltpu.CompilerParams(vmem_limit_bytes=48 * 1024 * 1024)


def dot_nn(a, b):
    return lax.dot_general(a, b, (((1,), (0,)), ((), ())), preferred_element_type=F32)


def dot_nt(a, b):
    return lax.dot_general(a, b, (((1,), (1,)), ((), ())), preferred_element_type=F32)


def dot_tn(a, b):
    return lax.dot_general(a, b, (((0,), (0,)), ((), ())), preferred_element_type=F32)


def running_sum(values):
    rows = values.shape[0]
    ids = lax.broadcasted_iota(jnp.int32, values.shape, 0)
    shift = 1
    while shift < rows:
        moved = pltpu.roll(values, shift, 0)
        values = values + jnp.where(ids >= shift, moved, 0.0)
        shift *= 2
    return values


def split_three(values):
    high = values.astype(BF16)
    rest = values - high.astype(F32)
    mid = rest.astype(BF16)
    low = (rest - mid.astype(F32)).astype(BF16)
    return high, mid, low


def projection(head, field_out):
    first = jnp.where(lax.broadcasted_iota(jnp.int32, (1, head.shape[0]), 1) == 0, 1.0, 0.0).astype(BF16)
    density = dot_nt(first, field_out)
    high, mid, low = split_three(head.T)
    proj = dot_nt(high, field_out) + (dot_nt(mid, field_out) + dot_nt(low, field_out))
    proj_high = proj.astype(BF16).astype(F32)
    rest = proj - proj_high
    return jnp.concatenate([density, proj_high, rest, jnp.zeros_like(density)], axis=0)


def forward_kernel(
    slab_ref, x_ref, spacing_ref, counts_ref, first_ref, last_ref, direction_ref,
    w1_ref, w2_ref, w3_ref, head_ref,
    seg_ref, h1_ref, h2_ref, save_ref, w8_ref, out8,
):
    samples, rays, _ = x_ref.shape
    w8 = projection(head_ref[...], w3_ref[...])
    w8_ref[...] = w8
    w16 = jnp.concatenate([w8, jnp.zeros_like(w8)], axis=0).astype(BF16)
    w1 = w1_ref[...]
    w2 = w2_ref[...]

    def step(j, carry):
        x = x_ref[j]
        h1 = jnp.maximum(dot_nn(x, w1), 0.0).astype(BF16)
        h1_ref[j] = h1
        h2 = jnp.maximum(dot_nn(h1, w2), 0.0).astype(BF16)
        h2_ref[j] = h2
        out8[j] = dot_nt(w16, h2)[:8]
        return carry

    lax.fori_loop(0, samples, step, 0, unroll=2)

    slab = slab_ref[0]
    density = out8[:, 0, :]
    proj = [out8[:, 1 + k, :] + out8[:, 4 + k, :] for k in range(3)]
    ids = lax.broadcasted_iota(jnp.int32, density.shape, 0)
    active = (first_ref[...] <= slab) & (slab < last_ref[...])
    live = jnp.where((ids < counts_ref[...]) & active, 1.0, 0.0)
    span = spacing_ref[...] * live
    optical = (jnp.maximum(density, 0.0) + jnp.log1p(jnp.exp(-jnp.abs(density)))) * span
    running = running_sum(optical)
    column = running[samples - 1 : samples]
    before = jnp.where(direction_ref[...] > 0, column - running, running - optical)
    reach = jnp.exp(-before)
    passed = jnp.exp(-optical)
    weights = reach * (1.0 - passed)
    seg_ref[...] = jnp.concatenate(
        [jnp.exp(-column)] + [jnp.sum(weights * p, axis=0, keepdims=True) for p in proj], axis=0
    )
    save_ref[0] = weights
    save_ref[1] = reach * passed
    save_ref[2] = span * jax.nn.sigmoid(density)
    for k in range(3):
        save_ref[3 + k] = proj[k]


def backward_kernel(
    ids_ref, x_ref, h1_ref, h2_ref, save_ref, w8_ref, w2_ref, head_ref, target_ref, direction_ref, *refs,
    n_pieces, n_slab,
):
    pieces = refs[:n_pieces]
    front_ref, keep_ref, send_ref, every, q8, acc = refs[n_pieces:]
    samples, rays, _ = x_ref.shape
    slab = ids_ref[0]
    core = ids_ref[1]
    at = 0
    for piece in pieces:
        if len(piece.shape) == 2:
            every[at] = piece[...]
            at += 1
        else:
            for i in range(piece.shape[0]):
                every[at + i] = piece[i]
            at += piece.shape[0]
    forward_ray = direction_ref[...] <= 0

    one = jnp.ones((1, rays), F32)
    zero = jnp.zeros((3, rays), F32)

    def compose(ascending):
        trans, color = one, zero
        order = range(n_slab) if ascending else range(n_slab - 1, -1, -1)
        early = forward_ray if ascending else jnp.logical_not(forward_ray)
        for s in order:
            item = every[jnp.bitwise_xor(slab, s)]
            keep = (s < slab) if ascending else (s > slab)
            item_trans = jnp.where(keep, item[0:1], 1.0)
            item_color = jnp.where(keep, item[1:4], 0.0)
            color = jnp.where(early, color + trans * item_color, item_color + item_trans * color)
            trans = trans * item_trans
        return trans, color

    low_trans, low_color = compose(True)
    high_trans, high_color = compose(False)
    front_trans = jnp.where(forward_ray, low_trans, high_trans)
    front_color = jnp.where(forward_ray, low_color, high_color)
    back_color = jnp.where(forward_ray, high_color, low_color)
    front_ref[...] = front_trans
    own = every[0]
    own_trans = own[0:1]
    logits = front_color + front_trans * own[1:4] + (front_trans * own_trans) * back_color
    shade = jax.nn.sigmoid(logits)
    error = (shade - target_ref[...].T) / rays
    grad_logit = error * shade * (1.0 - shade)
    grad_trans = front_trans * jnp.sum(grad_logit * back_color, axis=0, keepdims=True)
    pull = front_trans * grad_logit

    weights = save_ref[0]
    grad_weight = pull[0:1] * save_ref[3] + pull[1:2] * save_ref[4] + pull[2:3] * save_ref[5]
    product = weights * grad_weight
    running = running_sum(product)
    total = running[samples - 1 : samples]
    after = jnp.where(forward_ray, total - running, running - product)
    grad_optical = grad_weight * save_ref[1] - after - grad_trans * own_trans
    q8[:, 0, :] = grad_optical * save_ref[2]
    for k in range(3):
        q = weights * pull[k : k + 1]
        q8[:, 1 + k, :] = q
        q8[:, 4 + k, :] = q
    q8[:, 7, :] = jnp.zeros_like(weights)

    w8 = w8_ref[...]
    w16 = jnp.concatenate([w8, w8], axis=0).astype(BF16)
    w2 = w2_ref[...]
    acc[...] = jnp.zeros_like(acc)
    half_mid = w2.shape[0] // 2
    half_in = x_ref.shape[2] // 2
    rows_in = half_mid + half_in

    def step(j, carry):
        rows = q8[j]
        high = rows.astype(BF16).astype(F32)
        q16 = jnp.concatenate([high, rows - high], axis=0).astype(BF16)
        h1 = h1_ref[j]
        h2 = h2_ref[j]
        x = x_ref[j]
        grad_out = dot_nn(q16, h2)
        back_two = jnp.where(h2 > 0, dot_tn(q16, w16), 0.0).astype(BF16)
        grad_mid = dot_tn(h1, back_two)
        back_one = jnp.where(h1 > 0, dot_nt(back_two, w2), 0.0).astype(BF16)
        grad_in = dot_tn(x, back_one)
        for h in range(2):
            acc[h, :half_mid] += grad_mid[h * half_mid : (h + 1) * half_mid]
            acc[h, half_mid:rows_in] += grad_in[h * half_in : (h + 1) * half_in]
        acc[0, rows_in:] += grad_out[:8] + grad_out[8:]
        return carry

    lax.fori_loop(0, samples, step, 0, unroll=2)
    keep_ref[...] = acc[core]
    send_ref[...] = acc[1 - core]


def final_kernel(core_ref, own_ref, other_ref, head_ref, in_ref, mid_ref, out_ref):
    core = core_ref[0]
    half_mid = mid_ref.shape[0] // 2
    half_in = in_ref.shape[0] // 2
    rows_in = half_mid + half_in
    for h in range(2):

        def place(source):
            mid_ref[h * half_mid : (h + 1) * half_mid] = source[:half_mid]
            in_ref[h * half_in : (h + 1) * half_in] = source[half_mid:rows_in]
            if h == 0:
                factors = source[rows_in:]
                head = head_ref[...].T
                first = jnp.where(lax.broadcasted_iota(jnp.int32, (1, head.shape[1]), 1) == 0, 1.0, 0.0)
                rows = jnp.concatenate([first, head, jnp.zeros((4, head.shape[1]), F32)], axis=0)
                out_ref[...] = lax.dot_general(
                    factors, rows, (((0,), (0,)), ((), ())),
                    preferred_element_type=F32, precision=lax.Precision.HIGHEST,
                )

        pl.when(core == h)(functools.partial(place, own_ref))
        pl.when(core != h)(functools.partial(place, other_ref))


def pairs(size, bit):
    return [(i, i ^ bit) for i in range(size)]


def make_body(n_slab, n_tile):

    def body(
        encoded, spacing, counts, seg_first, seg_last, direction,
        field_in, field_mid, field_out, color_head, target,
    ):
        _, samples, rays, width = encoded.shape
        hidden = field_mid.shape[1]
        slab = lax.axis_index("slab")
        tile = lax.axis_index("tile")
        core = tile % 2
        x = encoded[0]
        row = lambda a: a.reshape(1, rays)
        w1, w2, w3 = field_in[0], field_mid[0], field_out[0]
        ids = jnp.stack([slab, core]).astype(jnp.int32)
        seg, h1, h2, save, w8 = pl.pallas_call(
            forward_kernel,
            name="forward",
            out_shape=(
                jax.ShapeDtypeStruct((4, rays), F32),
                jax.ShapeDtypeStruct((samples, rays, hidden), BF16),
                jax.ShapeDtypeStruct((samples, rays, hidden), BF16),
                jax.ShapeDtypeStruct((6, samples, rays), F32),
                jax.ShapeDtypeStruct((8, hidden), F32),
            ),
            in_specs=[SMEM] + [VMEM] * 10,
            out_specs=(VMEM,) * 5,
            scratch_shapes=[pltpu.VMEM((samples, 8, rays), F32)],
            compiler_params=LIMIT,
        )(ids, x, spacing[0], counts, row(seg_first), row(seg_last), row(direction), w1, w2, w3, color_head)

        pieces = [seg]
        known = seg[None]
        bit = 1
        while bit < n_slab:
            got = lax.ppermute(known, "slab", pairs(n_slab, bit))
            pieces.append(got)
            bit *= 2
            if bit < n_slab:
                known = jnp.concatenate([known, got], axis=0)

        half = (hidden + width) // 2 + 8
        front, keep, send = pl.pallas_call(
            functools.partial(backward_kernel, n_pieces=len(pieces), n_slab=n_slab),
            name="backward",
            out_shape=(
                jax.ShapeDtypeStruct((1, rays), F32),
                jax.ShapeDtypeStruct((half, hidden), F32),
                jax.ShapeDtypeStruct((half, hidden), F32),
            ),
            in_specs=[SMEM] + [VMEM] * (9 + len(pieces)),
            out_specs=(VMEM,) * 3,
            scratch_shapes=[
                pltpu.VMEM((n_slab, 4, rays), F32),
                pltpu.VMEM((samples, 8, rays), F32),
                pltpu.VMEM((2, half, hidden), F32),
            ],
            compiler_params=LIMIT,
        )(ids, x, h1, h2, save, w8, w2, color_head, target, row(direction), *pieces)

        part = keep + lax.ppermute(send, "tile", pairs(n_tile, 1))
        bit = 2
        while bit < n_tile:
            part = part + lax.ppermute(part, "tile", pairs(n_tile, bit))
            bit *= 2
        other = lax.ppermute(part, "tile", pairs(n_tile, 1))
        grad_in, grad_mid, grad_out = pl.pallas_call(
            final_kernel,
            name="final",
            out_shape=(
                jax.ShapeDtypeStruct(w1.shape, F32),
                jax.ShapeDtypeStruct(w2.shape, F32),
                jax.ShapeDtypeStruct(w3.shape, F32),
            ),
            in_specs=[SMEM] + [VMEM] * 3,
            out_specs=(VMEM,) * 3,
            compiler_params=LIMIT,
        )(core.reshape(1).astype(jnp.int32), part, other, color_head)
        return front, grad_in[None], grad_mid[None], grad_out[None]

    return body


def solution(mesh):
    return jax.shard_map(
        make_body(mesh.shape["slab"], mesh.shape["tile"]),
        mesh=mesh,
        in_specs=(
            P("slab", None, "tile", None),
            P("slab", None, "tile"),
            P("slab", "tile"),
            P("tile"),
            P("tile"),
            P("tile"),
            P("slab", None, None),
            P("slab", None, None),
            P("slab", None, None),
            P(),
            P("tile", None),
        ),
        out_specs=(
            P("slab", "tile"),
            P("slab", None, None),
            P("slab", None, None),
            P("slab", None, None),
        ),
        check_vma=False,
    )
```

```python
import functools

import jax
import jax.numpy as jnp
from jax import lax
from jax.experimental import pallas as pl
from jax.experimental.pallas import tpu as pltpu
from jax.sharding import PartitionSpec as P

F32 = jnp.float32
BF16 = jnp.bfloat16
VMEM = pl.BlockSpec(memory_space=pltpu.VMEM)
SMEM = pl.BlockSpec(memory_space=pltpu.SMEM)
HBM = pl.BlockSpec(memory_space=pltpu.HBM)
LIMIT = pltpu.CompilerParams(vmem_limit_bytes=32 * 1024 * 1024)
CHUNKS = 4


def dot_nn(a, b):
    return lax.dot_general(a, b, (((1,), (0,)), ((), ())), preferred_element_type=F32)


def dot_nt(a, b):
    return lax.dot_general(a, b, (((1,), (1,)), ((), ())), preferred_element_type=F32)


def dot_tn(a, b):
    return lax.dot_general(a, b, (((0,), (0,)), ((), ())), preferred_element_type=F32)


def running_sum(values):
    rows = values.shape[0]
    ids = lax.broadcasted_iota(jnp.int32, values.shape, 0)
    shift = 1
    while shift < rows:
        moved = pltpu.roll(values, shift, 0)
        values = values + jnp.where(ids >= shift, moved, 0.0)
        shift *= 2
    return values


def split_three(values):
    high = values.astype(BF16)
    rest = values - high.astype(F32)
    mid = rest.astype(BF16)
    low = (rest - mid.astype(F32)).astype(BF16)
    return high, mid, low


def projection(head, field_out):
    first = jnp.where(lax.broadcasted_iota(jnp.int32, (1, head.shape[1]), 1) == 0, 1.0, 0.0).astype(BF16)
    density = dot_nn(first, field_out)
    high, mid, low = split_three(head)
    proj = dot_nn(high, field_out) + (dot_nn(mid, field_out) + dot_nn(low, field_out))
    proj_high = proj.astype(BF16).astype(F32)
    rest = proj - proj_high
    eight = jnp.concatenate([density, proj_high, rest, jnp.zeros_like(density)], axis=0)
    return jnp.concatenate([eight, eight], axis=0).astype(BF16)


def positive(values):
    rounded = values.astype(BF16)
    return jnp.maximum(rounded, jnp.zeros_like(rounded))


def where_positive(mask, values):
    rounded = values.astype(BF16)
    return jnp.where(mask > 0, rounded, jnp.zeros_like(rounded))


def forward_kernel(
    slab_ref, x_hbm, spacing_hbm, counts_hbm, first_hbm, last_hbm, direction_hbm, target_hbm,
    w1_hbm, w2_hbm, w3_hbm, head_hbm,
    seg_ref, x_ref, h1_ref, h2_ref, save_ref, w16_ref, w2_ref, direction_ref, target_ref,
    w1_ref, w3_ref, head_ref, spacing_ref, counts_ref, first_ref, last_ref, out8, sems,
):
    samples, _, rays = out8.shape
    count = x_ref.shape[0]
    chunk = count // CHUNKS
    moves = [
        pltpu.make_async_copy(source, place, sems.at[i])
        for i, (source, place) in enumerate(
            (
                (head_hbm, head_ref), (w3_hbm, w3_ref), (w1_hbm, w1_ref), (w2_hbm, w2_ref),
                (spacing_hbm, spacing_ref), (counts_hbm, counts_ref), (first_hbm, first_ref),
                (last_hbm, last_ref), (direction_hbm, direction_ref), (target_hbm, target_ref),
            )
        )
    ]
    loads = [
        pltpu.make_async_copy(
            x_hbm.at[pl.ds(c * chunk, chunk)], x_ref.at[pl.ds(c * chunk, chunk)], sems.at[len(moves) + c]
        )
        for c in range(CHUNKS)
    ]
    for move in moves[:3] + loads[:1] + moves[3:4] + loads[1:] + moves[4:]:
        move.start()
    moves[0].wait()
    moves[1].wait()
    w16_ref[...] = projection(head_ref[...], w3_ref[...])
    moves[2].wait()
    moves[3].wait()

    for c in range(CHUNKS):
        loads[c].wait()
        rows = pl.ds(c * chunk, chunk)
        h1 = positive(dot_nn(x_ref[rows], w1_ref[...]))
        h1_ref[rows] = h1
        h2 = positive(dot_nn(h1, w2_ref[...]))
        h2_ref[rows] = h2
        eight = dot_nt(w16_ref[...], h2)[:8]
        each = chunk // rays
        for j in range(each):
            out8[c * each + j] = eight[:, j * rays : (j + 1) * rays]

    for move in moves[4:]:
        move.wait()
    slab = slab_ref[0]
    density = out8[:, 0, :]
    proj = [out8[:, 1 + k, :] + out8[:, 4 + k, :] for k in range(3)]
    ids = lax.broadcasted_iota(jnp.int32, density.shape, 0)
    active = (first_ref[...] <= slab) & (slab < last_ref[...])
    live = jnp.where((ids < counts_ref[...]) & active, 1.0, 0.0)
    span = spacing_ref[...] * live
    optical = (jnp.maximum(density, 0.0) + jnp.log1p(jnp.exp(-jnp.abs(density)))) * span
    running = running_sum(optical)
    column = running[samples - 1 : samples]
    before = jnp.where(direction_ref[...] > 0, column - running, running - optical)
    reach = jnp.exp(-before)
    passed = jnp.exp(-optical)
    weights = reach * (1.0 - passed)
    seg_ref[...] = jnp.concatenate(
        [jnp.exp(-column)] + [jnp.sum(weights * p, axis=0, keepdims=True) for p in proj], axis=0
    )
    save_ref[0] = weights
    save_ref[1] = reach * passed
    save_ref[2] = span * jax.nn.sigmoid(density)
    for k in range(3):
        save_ref[3 + k] = proj[k]


def backward_kernel(
    ids_ref, x_ref, h1_ref, h2_ref, save_ref, w16_ref, w2_ref, direction_ref, target_ref, *refs,
    n_pieces, n_slab,
):
    pieces = refs[:n_pieces]
    front_hbm, keep_ref, send_ref, front_ref, every, q8, q16, mid_ref, in_ref, out_ref, sem = refs[n_pieces:]
    samples, _, rays = q8.shape
    count = x_ref.shape[0]
    slab = ids_ref[0]
    core = ids_ref[1]
    at = 0
    for piece in pieces:
        for i in range(piece.shape[0]):
            every[at + i] = piece[i]
        at += piece.shape[0]
    forward_ray = direction_ref[...] <= 0

    one = jnp.ones((1, rays), F32)
    zero = jnp.zeros((3, rays), F32)

    def compose(ascending):
        trans, color = one, zero
        order = range(n_slab) if ascending else range(n_slab - 1, -1, -1)
        early = forward_ray if ascending else jnp.logical_not(forward_ray)
        for s in order:
            item = every[jnp.bitwise_xor(slab, s)]
            keep = (s < slab) if ascending else (s > slab)
            item_trans = jnp.where(keep, item[0:1], 1.0)
            item_color = jnp.where(keep, item[1:4], 0.0)
            color = jnp.where(early, color + trans * item_color, item_color + item_trans * color)
            trans = trans * item_trans
        return trans, color

    low_trans, low_color = compose(True)
    high_trans, high_color = compose(False)
    front_trans = jnp.where(forward_ray, low_trans, high_trans)
    front_color = jnp.where(forward_ray, low_color, high_color)
    back_color = jnp.where(forward_ray, high_color, low_color)
    front_ref[...] = front_trans
    store = pltpu.make_async_copy(front_ref, front_hbm, sem)
    store.start()
    own = every[0]
    own_trans = own[0:1]
    logits = front_color + front_trans * own[1:4] + (front_trans * own_trans) * back_color
    shade = jax.nn.sigmoid(logits)
    error = (shade - target_ref[...]) / rays
    grad_logit = error * shade * (1.0 - shade)
    grad_trans = front_trans * jnp.sum(grad_logit * back_color, axis=0, keepdims=True)
    pull = front_trans * grad_logit

    weights = save_ref[0]
    grad_weight = pull[0:1] * save_ref[3] + pull[1:2] * save_ref[4] + pull[2:3] * save_ref[5]
    product = weights * grad_weight
    running = running_sum(product)
    total = running[samples - 1 : samples]
    after = jnp.where(forward_ray, total - running, running - product)
    grad_optical = grad_weight * save_ref[1] - after - grad_trans * own_trans
    q8[:, 0, :] = grad_optical * save_ref[2]
    for k in range(3):
        q = weights * pull[k : k + 1]
        q8[:, 1 + k, :] = q
        q8[:, 4 + k, :] = q
    q8[:, 7, :] = jnp.zeros_like(weights)
    for j in range(samples):
        rows = q8[j]
        high = rows.astype(BF16).astype(F32)
        q16[:, j * rays : (j + 1) * rays] = jnp.concatenate([high, rows - high], axis=0).astype(BF16)

    chunk = count // CHUNKS
    for c in range(CHUNKS):
        rows = pl.ds(c * chunk, chunk)
        q = q16[:, rows]
        h1 = h1_ref[rows]
        h2 = h2_ref[rows]
        back_two = where_positive(h2, dot_tn(q, w16_ref[...]))
        grad_out = dot_nn(q, h2)
        grad_mid = dot_tn(h1, back_two)
        back_one = where_positive(h1, dot_nt(back_two, w2_ref[...]))
        grad_in = dot_tn(x_ref[rows], back_one)
        for ref, part in ((out_ref, grad_out), (mid_ref, grad_mid), (in_ref, grad_in)):
            ref[...] = part if c == 0 else ref[...] + part

    half_mid = mid_ref.shape[0] // 2
    half_in = in_ref.shape[0] // 2
    rows_in = half_mid + half_in
    for place, half in ((send_ref, 1 - core), (keep_ref, core)):
        place[:half_mid] = mid_ref[pl.ds(pl.multiple_of(half * half_mid, half_mid), half_mid)]
        place[half_mid:rows_in] = in_ref[pl.ds(pl.multiple_of(half * half_in, half_in), half_in)]
        place[rows_in:] = out_ref[:8] + out_ref[8:]
    store.wait()


def final_kernel(core_ref, own_ref, other_ref, head_ref, in_hbm, mid_hbm, out_hbm, out_ref, sems):
    core = core_ref[0]
    half_mid = mid_hbm.shape[0] // 2
    half_in = in_hbm.shape[0] // 2
    rows_in = half_mid + half_in
    moves = []
    for source, half in ((own_ref, core), (other_ref, 1 - core)):
        for start, size, place in ((0, half_mid, mid_hbm), (half_mid, half_in, in_hbm)):
            moves.append(
                pltpu.make_async_copy(
                    source.at[pl.ds(start, size)],
                    place.at[pl.ds(pl.multiple_of(half * size, size), size)],
                    sems.at[len(moves)],
                )
            )
    for move in moves:
        move.start()
    factors = own_ref[rows_in:]
    head = head_ref[...]
    width = head.shape[1]
    first = jnp.where(lax.broadcasted_iota(jnp.int32, (1, width), 1) == 0, 1.0, 0.0)
    rows = jnp.concatenate([first, head, jnp.zeros((4, width), F32)], axis=0)
    out_ref[...] = lax.dot_general(
        rows, factors, (((0,), (0,)), ((), ())), preferred_element_type=F32, precision=lax.Precision.HIGHEST
    )
    moves.append(pltpu.make_async_copy(out_ref, out_hbm, sems.at[len(moves)]))
    moves[-1].start()
    for move in moves:
        move.wait()


def pairs(size, bit):
    return [(i, i ^ bit) for i in range(size)]


def make_body(n_slab, n_tile):

    def body(
        encoded, spacing, counts, seg_first, seg_last, direction,
        field_in, field_mid, field_out, color_head, target,
    ):
        _, samples, rays, width = encoded.shape
        hidden = field_mid.shape[1]
        features = field_out.shape[2]
        count = samples * rays
        slab = lax.axis_index("slab")
        core = lax.axis_index("tile") % 2
        row = lambda a: a.reshape(1, rays)
        ids = jnp.stack([slab, core]).astype(jnp.int32)
        seg, *kept = pl.pallas_call(
            forward_kernel,
            name="forward",
            out_shape=(
                pltpu.VMEM((4, rays), F32),
                pltpu.VMEM((count, width), BF16),
                pltpu.VMEM((count, hidden), BF16),
                pltpu.VMEM((count, hidden), BF16),
                pltpu.VMEM((6, samples, rays), F32),
                pltpu.VMEM((16, hidden), BF16),
                pltpu.VMEM((hidden, hidden), BF16),
                pltpu.VMEM((1, rays), jnp.int32),
                pltpu.VMEM((3, rays), F32),
            ),
            in_specs=[SMEM] + [HBM] * 11,
            out_specs=(VMEM,) * 9,
            scratch_shapes=[
                pltpu.VMEM((width, hidden), BF16),
                pltpu.VMEM((features, hidden), BF16),
                pltpu.VMEM((3, features), F32),
                pltpu.VMEM((samples, rays), F32),
                pltpu.VMEM((1, rays), jnp.int32),
                pltpu.VMEM((1, rays), jnp.int32),
                pltpu.VMEM((1, rays), jnp.int32),
                pltpu.VMEM((samples, 8, rays), F32),
                pltpu.SemaphoreType.DMA((10 + CHUNKS,)),
            ],
            compiler_params=LIMIT,
        )(
            ids,
            *(
                pltpu.with_memory_space_constraint(a, pltpu.HBM)
                for a in (
                    encoded[0].reshape(count, width), spacing[0], counts, row(seg_first), row(seg_last),
                    row(direction), target.T, field_in[0], field_mid[0], field_out[0].T, color_head.T,
                )
            ),
        )

        known = seg[None]
        pieces = [known]
        bit = 1
        while bit < n_slab:
            got = lax.ppermute(known, "slab", pairs(n_slab, bit))
            pieces.append(got)
            bit *= 2
            if bit < n_slab:
                known = jnp.concatenate([known, got], axis=0)

        half = (hidden + width) // 2 + 8
        front, keep, send = pl.pallas_call(
            functools.partial(backward_kernel, n_pieces=len(pieces), n_slab=n_slab),
            name="backward",
            out_shape=(
                pltpu.HBM((1, rays), F32),
                pltpu.VMEM((half, hidden), F32),
                pltpu.VMEM((half, hidden), F32),
            ),
            in_specs=[SMEM] + [VMEM] * (8 + len(pieces)),
            out_specs=(HBM, VMEM, VMEM),
            scratch_shapes=[
                pltpu.VMEM((1, rays), F32),
                pltpu.VMEM((n_slab, 4, rays), F32),
                pltpu.VMEM((samples, 8, rays), F32),
                pltpu.VMEM((16, count), BF16),
                pltpu.VMEM((hidden, hidden), F32),
                pltpu.VMEM((width, hidden), F32),
                pltpu.VMEM((16, hidden), F32),
                pltpu.SemaphoreType.DMA,
            ],
            compiler_params=LIMIT,
        )(ids, *kept, *pieces)

        part = keep + lax.ppermute(send, "tile", pairs(n_tile, 1))
        bit = 2
        while bit < n_tile:
            part = part + lax.ppermute(part, "tile", pairs(n_tile, bit))
            bit *= 2
        other = lax.ppermute(part, "tile", pairs(n_tile, 1))
        grad_in, grad_mid, grad_out = pl.pallas_call(
            final_kernel,
            name="final",
            out_shape=(
                pltpu.HBM((width, hidden), F32),
                pltpu.HBM((hidden, hidden), F32),
                pltpu.HBM((features, hidden), F32),
            ),
            in_specs=[SMEM] + [VMEM] * 3,
            out_specs=(HBM,) * 3,
            scratch_shapes=[pltpu.VMEM((features, hidden), F32), pltpu.SemaphoreType.DMA((5,))],
            compiler_params=LIMIT,
        )(core.reshape(1).astype(jnp.int32), part, other, color_head.T)
        return front, grad_in[None], grad_mid[None], grad_out.T[None]

    return body


def solution(mesh):
    return jax.shard_map(
        make_body(mesh.shape["slab"], mesh.shape["tile"]),
        mesh=mesh,
        in_specs=(
            P("slab", None, "tile", None),
            P("slab", None, "tile"),
            P("slab", "tile"),
            P("tile"),
            P("tile"),
            P("tile"),
            P("slab", None, None),
            P("slab", None, None),
            P("slab", None, None),
            P(),
            P("tile", None),
        ),
        out_specs=(
            P("slab", "tile"),
            P("slab", None, None),
            P("slab", None, None),
            P("slab", None, None),
        ),
        check_vma=False,
    )
```

```python
import functools

import jax
import jax.numpy as jnp
from jax import lax
from jax.experimental import pallas as pl
from jax.experimental.pallas import tpu as pltpu
from jax.sharding import PartitionSpec as P

F32 = jnp.float32
BF16 = jnp.bfloat16
VMEM = pl.BlockSpec(memory_space=pltpu.VMEM)
HBM = pl.BlockSpec(memory_space=pltpu.HBM)
LIMIT = pltpu.CompilerParams(vmem_limit_bytes=32 * 1024 * 1024)
FORWARD_CHUNKS = 4
BACKWARD_CHUNKS = 8


def dot_nn(a, b):
    return lax.dot_general(a, b, (((1,), (0,)), ((), ())), preferred_element_type=F32)


def dot_nt(a, b):
    return lax.dot_general(a, b, (((1,), (1,)), ((), ())), preferred_element_type=F32)


def dot_tn(a, b):
    return lax.dot_general(a, b, (((0,), (0,)), ((), ())), preferred_element_type=F32)


def running_sum(values):
    rows = values.shape[0]
    ids = lax.broadcasted_iota(jnp.int32, values.shape, 0)
    shift = 1
    while shift < rows:
        moved = pltpu.roll(values, shift, 0)
        values = values + jnp.where(ids >= shift, moved, 0.0)
        shift *= 2
    return values


def split_three(values):
    high = values.astype(BF16)
    rest = values - high.astype(F32)
    mid = rest.astype(BF16)
    low = (rest - mid.astype(F32)).astype(BF16)
    return high, mid, low


def projection(head, field_out):
    first = jnp.where(lax.broadcasted_iota(jnp.int32, (1, head.shape[1]), 1) == 0, 1.0, 0.0).astype(BF16)
    density = dot_nn(first, field_out)
    high, mid, low = split_three(head)
    proj = dot_nn(high, field_out) + (dot_nn(mid, field_out) + dot_nn(low, field_out))
    proj_high = proj.astype(BF16).astype(F32)
    rest = proj - proj_high
    eight = jnp.concatenate([density, proj_high, rest, jnp.zeros_like(density)], axis=0)
    return jnp.concatenate([eight, eight], axis=0).astype(BF16)


def positive(values):
    rounded = values.astype(BF16)
    return jnp.maximum(rounded, jnp.zeros_like(rounded))


def where_positive(mask, values):
    rounded = values.astype(BF16)
    return jnp.where(mask > 0, rounded, jnp.zeros_like(rounded))


def forward_kernel(
    x_hbm, spacing_hbm, counts_hbm, first_hbm, last_hbm, direction_hbm, target_hbm,
    w1_hbm, w2_hbm, w3_hbm, head_hbm,
    seg_ref, order_ref, x_ref, h1_ref, h2_ref, save_ref, w16_ref, w2_ref, target_ref,
    w1_ref, w3_ref, head_ref, spacing_ref, counts_ref, first_ref, last_ref, direction_ref, out8, sems,
):
    samples, _, rays = out8.shape
    count = x_ref.shape[0]
    chunk = count // FORWARD_CHUNKS
    moves = [
        pltpu.make_async_copy(source, place, sems.at[i])
        for i, (source, place) in enumerate(
            (
                (head_hbm, head_ref), (w3_hbm, w3_ref), (w1_hbm, w1_ref), (w2_hbm, w2_ref),
                (spacing_hbm, spacing_ref), (counts_hbm, counts_ref), (first_hbm, first_ref),
                (last_hbm, last_ref), (direction_hbm, direction_ref), (target_hbm, target_ref),
            )
        )
    ]
    loads = [
        pltpu.make_async_copy(x_hbm.at[pl.ds(at, size)], x_ref.at[pl.ds(at, size)], sems.at[len(moves) + i])
        for i, (at, size) in enumerate(((0, chunk), (chunk, count - chunk)))
    ]
    for move in moves[:3] + loads[:1] + moves[3:4] + loads[1:] + moves[4:]:
        move.start()
    moves[0].wait()
    moves[1].wait()
    w16_ref[...] = projection(head_ref[...], w3_ref[...])
    moves[2].wait()
    moves[3].wait()

    for c in range(FORWARD_CHUNKS):
        if c < 2:
            loads[c].wait()
        rows = pl.ds(c * chunk, chunk)
        h1 = positive(dot_nn(x_ref[rows], w1_ref[...]))
        h1_ref[rows] = h1
        h2 = positive(dot_nn(h1, w2_ref[...]))
        h2_ref[rows] = h2
        eight = dot_nt(w16_ref[...], h2)[:8]
        each = chunk // rays
        for j in range(each):
            out8[c * each + j] = eight[:, j * rays : (j + 1) * rays]

    for move in moves[4:]:
        move.wait()
    slab = lax.axis_index("slab")
    reverse = jnp.minimum(jnp.maximum(direction_ref[...], 0), 1)
    for bit in range(order_ref.shape[0]):
        higher = (slab >> bit) & 1
        order_ref[bit] = 1 - (reverse ^ higher)
    density = out8[:, 0, :]
    proj = [out8[:, 1 + k, :] + out8[:, 4 + k, :] for k in range(3)]
    ids = lax.broadcasted_iota(jnp.int32, density.shape, 0)
    active = (first_ref[...] <= slab) & (slab < last_ref[...])
    live = jnp.where((ids < counts_ref[...]) & active, 1.0, 0.0)
    span = spacing_ref[...] * live
    optical = (jnp.maximum(density, 0.0) + jnp.log1p(jnp.exp(-jnp.abs(density)))) * span
    running = running_sum(optical)
    column = running[samples - 1 : samples]
    before = jnp.where(direction_ref[...] > 0, column - running, running - optical)
    reach = jnp.exp(-before)
    passed = jnp.exp(-optical)
    weights = reach * (1.0 - passed)
    seg_ref[...] = jnp.concatenate(
        [jnp.exp(-column)] + [jnp.sum(weights * p, axis=0, keepdims=True) for p in proj], axis=0
    )
    save_ref[0] = weights
    save_ref[1] = reach * passed
    save_ref[2] = span * jax.nn.sigmoid(density)
    for k in range(3):
        save_ref[3 + k] = proj[k]


def backward_kernel(
    own_ref, order_ref, x_ref, h1_ref, h2_ref, save_ref, w16_ref, w2_ref, target_ref, *refs, n_tile,
):
    n_bits = order_ref.shape[0]
    pieces = refs[:n_bits]
    front_hbm, keep_ref, send_ref, front_ref, q8, q16, mid_ref, in_ref, out_ref, sem = refs[n_bits:]
    samples, _, rays = q8.shape
    count = x_ref.shape[0]
    slab = lax.axis_index("slab")
    kept = kept_half(lax.axis_index("tile"), n_tile)

    front_trans = back_trans = jnp.ones((1, rays), F32)
    front_color = back_color = jnp.zeros((3, rays), F32)
    for bit in range(n_bits):
        behind = order_ref[bit] > 0
        trans, color = pieces[bit][0:1], pieces[bit][1:4]
        front_color = jnp.where(behind, front_color, color + trans * front_color)
        front_trans = jnp.where(behind, front_trans, trans * front_trans)
        back_color = jnp.where(behind, back_color + back_trans * color, back_color)
        back_trans = jnp.where(behind, back_trans * trans, back_trans)
    forward_ray = (order_ref[0] ^ (slab & 1)) > 0
    front_ref[...] = front_trans
    store = pltpu.make_async_copy(front_ref, front_hbm, sem)
    store.start()
    own = own_ref[...]
    own_trans = own[0:1]
    logits = front_color + front_trans * own[1:4] + (front_trans * own_trans) * back_color
    shade = jax.nn.sigmoid(logits)
    error = (shade - target_ref[...]) / rays
    grad_logit = error * shade * (1.0 - shade)
    grad_trans = front_trans * jnp.sum(grad_logit * back_color, axis=0, keepdims=True)
    pull = front_trans * grad_logit

    weights = save_ref[0]
    grad_weight = pull[0:1] * save_ref[3] + pull[1:2] * save_ref[4] + pull[2:3] * save_ref[5]
    product = weights * grad_weight
    running = running_sum(product)
    total = running[samples - 1 : samples]
    after = jnp.where(forward_ray, total - running, running - product)
    grad_optical = grad_weight * save_ref[1] - after - grad_trans * own_trans
    q8[:, 0, :] = grad_optical * save_ref[2]
    for k in range(3):
        q = weights * pull[k : k + 1]
        q8[:, 1 + k, :] = q
        q8[:, 4 + k, :] = q
    q8[:, 7, :] = jnp.zeros_like(weights)
    for j in range(samples):
        rows = q8[j]
        high = rows.astype(BF16).astype(F32)
        q16[:, j * rays : (j + 1) * rays] = jnp.concatenate([high, rows - high], axis=0).astype(BF16)

    chunk = count // BACKWARD_CHUNKS
    for c in range(BACKWARD_CHUNKS):
        rows = pl.ds(c * chunk, chunk)
        q = q16[:, rows]
        h1 = h1_ref[rows]
        h2 = h2_ref[rows]
        back_two = where_positive(h2, dot_tn(q, w16_ref[...]))
        grad_out = dot_nn(q, h2)
        grad_mid = dot_tn(h1, back_two)
        back_one = where_positive(h1, dot_nt(back_two, w2_ref[...]))
        grad_in = dot_tn(x_ref[rows], back_one)
        for ref, part in ((out_ref, grad_out), (mid_ref, grad_mid), (in_ref, grad_in)):
            ref[...] = part if c == 0 else ref[...] + part

    half_mid = mid_ref.shape[0] // 2
    half_in = in_ref.shape[0] // 2
    rows_in = half_mid + half_in
    for place, half in ((send_ref, 1 - kept), (keep_ref, kept)):
        place[:half_mid] = mid_ref[pl.ds(pl.multiple_of(half * half_mid, half_mid), half_mid)]
        place[half_mid:rows_in] = in_ref[pl.ds(pl.multiple_of(half * half_in, half_in), half_in)]
        place[rows_in:] = out_ref[:8] + out_ref[8:]
    store.wait()


def final_kernel(own_ref, other_ref, head_ref, in_hbm, mid_hbm, out_hbm, out_ref, sems, *, n_tile):
    kept = kept_half(lax.axis_index("tile"), n_tile)
    half_mid = mid_hbm.shape[0] // 2
    half_in = in_hbm.shape[0] // 2
    rows_in = half_mid + half_in
    moves = []
    for source, half in ((own_ref, kept), (other_ref, 1 - kept)):
        for start, size, place in ((0, half_mid, mid_hbm), (half_mid, half_in, in_hbm)):
            moves.append(
                pltpu.make_async_copy(
                    source.at[pl.ds(start, size)],
                    place.at[pl.ds(pl.multiple_of(half * size, size), size)],
                    sems.at[len(moves)],
                )
            )
    for move in moves:
        move.start()
    factors = own_ref[rows_in:]
    head = head_ref[...]
    width = head.shape[1]
    first = jnp.where(lax.broadcasted_iota(jnp.int32, (1, width), 1) == 0, 1.0, 0.0)
    rows = jnp.concatenate([first, head, jnp.zeros((4, width), F32)], axis=0)
    out_ref[...] = lax.dot_general(
        rows, factors, (((0,), (0,)), ((), ())), preferred_element_type=F32, precision=lax.Precision.HIGHEST
    )
    moves.append(pltpu.make_async_copy(out_ref, out_hbm, sems.at[len(moves)]))
    moves[-1].start()
    for move in moves:
        move.wait()


def kept_half(tile, n_tile):
    half = tile & 1
    shift = 1
    while (1 << shift) < n_tile:
        half = half ^ ((tile >> shift) & 1)
        shift += 1
    return half


def joined(own, got, own_first):
    first = jnp.where(own_first, own, got)
    second = jnp.where(own_first, got, own)
    row = lax.broadcasted_iota(jnp.int32, own.shape, 0)
    return first[0:1] * second + jnp.where(row == 0, 0.0, first)


def pairs(size, bit):
    return [(i, i ^ bit) for i in range(size)]


def make_body(n_slab, n_tile):

    def body(
        encoded, spacing, counts, seg_first, seg_last, direction,
        field_in, field_mid, field_out, color_head, target,
    ):
        _, samples, rays, width = encoded.shape
        hidden = field_mid.shape[1]
        features = field_out.shape[2]
        count = samples * rays
        n_bits = (n_slab - 1).bit_length()
        row = lambda a: a.reshape(1, rays)
        seg, order, *kept = pl.pallas_call(
            forward_kernel,
            name="forward",
            out_shape=(
                pltpu.VMEM((4, rays), F32),
                pltpu.VMEM((n_bits, 1, rays), jnp.int32),
                pltpu.VMEM((count, width), BF16),
                pltpu.VMEM((count, hidden), BF16),
                pltpu.VMEM((count, hidden), BF16),
                pltpu.VMEM((6, samples, rays), F32),
                pltpu.VMEM((16, hidden), BF16),
                pltpu.VMEM((hidden, hidden), BF16),
                pltpu.VMEM((3, rays), F32),
            ),
            in_specs=[HBM] * 11,
            out_specs=(VMEM,) * 9,
            scratch_shapes=[
                pltpu.VMEM((width, hidden), BF16),
                pltpu.VMEM((features, hidden), BF16),
                pltpu.VMEM((3, features), F32),
                pltpu.VMEM((samples, rays), F32),
                pltpu.VMEM((1, rays), jnp.int32),
                pltpu.VMEM((1, rays), jnp.int32),
                pltpu.VMEM((1, rays), jnp.int32),
                pltpu.VMEM((1, rays), jnp.int32),
                pltpu.VMEM((samples, 8, rays), F32),
                pltpu.SemaphoreType.DMA((12,)),
            ],
            compiler_params=LIMIT,
        )(
            *(
                pltpu.with_memory_space_constraint(a, pltpu.HBM)
                for a in (
                    encoded[0].reshape(count, width), spacing[0], counts, row(seg_first), row(seg_last),
                    row(direction), target.T, field_in[0], field_mid[0], field_out[0].T, color_head.T,
                )
            ),
        )

        block = seg
        pieces = []
        for bit in range(n_bits):
            got = lax.ppermute(block, "slab", pairs(n_slab, 1 << bit))
            pieces.append(got)
            if bit + 1 < n_bits:
                block = joined(block, got, order[bit] > 0)

        half = (hidden + width) // 2 + 8
        front, keep, send = pl.pallas_call(
            functools.partial(backward_kernel, n_tile=n_tile),
            name="backward",
            out_shape=(
                pltpu.HBM((1, rays), F32),
                pltpu.VMEM((half, hidden), F32),
                pltpu.VMEM((half, hidden), F32),
            ),
            in_specs=[VMEM] * (9 + n_bits),
            out_specs=(HBM, VMEM, VMEM),
            scratch_shapes=[
                pltpu.VMEM((1, rays), F32),
                pltpu.VMEM((samples, 8, rays), F32),
                pltpu.VMEM((16, count), BF16),
                pltpu.VMEM((hidden, hidden), F32),
                pltpu.VMEM((width, hidden), F32),
                pltpu.VMEM((16, hidden), F32),
                pltpu.SemaphoreType.DMA,
            ],
            compiler_params=LIMIT,
        )(seg, order, *kept, *pieces)

        part = keep + lax.ppermute(send, "tile", pairs(n_tile, 1))
        bit = 2
        while bit < n_tile:
            part = part + lax.ppermute(part, "tile", pairs(n_tile, bit | 1))
            bit *= 2
        other = lax.ppermute(part, "tile", pairs(n_tile, 1))
        grad_in, grad_mid, grad_out = pl.pallas_call(
            functools.partial(final_kernel, n_tile=n_tile),
            name="final",
            out_shape=(
                pltpu.HBM((width, hidden), F32),
                pltpu.HBM((hidden, hidden), F32),
                pltpu.HBM((features, hidden), F32),
            ),
            in_specs=[VMEM] * 3,
            out_specs=(HBM,) * 3,
            scratch_shapes=[pltpu.VMEM((features, hidden), F32), pltpu.SemaphoreType.DMA((5,))],
            compiler_params=LIMIT,
        )(part, other, color_head.T)
        return front, grad_in[None], grad_mid[None], grad_out.T[None]

    return body


def solution(mesh):
    return jax.shard_map(
        make_body(mesh.shape["slab"], mesh.shape["tile"]),
        mesh=mesh,
        in_specs=(
            P("slab", None, "tile", None),
            P("slab", None, "tile"),
            P("slab", "tile"),
            P("tile"),
            P("tile"),
            P("tile"),
            P("slab", None, None),
            P("slab", None, None),
            P("slab", None, None),
            P(),
            P("tile", None),
        ),
        out_specs=(
            P("slab", "tile"),
            P("slab", None, None),
            P("slab", None, None),
            P("slab", None, None),
        ),
        check_vma=False,
    )
```

```python
import functools

import jax
import jax.numpy as jnp
from jax import lax
from jax.experimental import pallas as pl
from jax.experimental.pallas import tpu as pltpu
from jax.sharding import PartitionSpec as P

F32 = jnp.float32
BF16 = jnp.bfloat16
VMEM = pl.BlockSpec(memory_space=pltpu.VMEM)
HBM = pl.BlockSpec(memory_space=pltpu.HBM)
LIMIT = pltpu.CompilerParams(vmem_limit_bytes=32 * 1024 * 1024)
FORWARD_CHUNKS = 4
BACKWARD_CHUNKS = 8
INNER_CHUNKS = 8
FIRST_CHUNKS = 8


def dot_nn(a, b):
    return lax.dot_general(a, b, (((1,), (0,)), ((), ())), preferred_element_type=F32)


def dot_nt(a, b):
    return lax.dot_general(a, b, (((1,), (1,)), ((), ())), preferred_element_type=F32)


def dot_tn(a, b):
    return lax.dot_general(a, b, (((0,), (0,)), ((), ())), preferred_element_type=F32)


def running_sum(values):
    rows = values.shape[0]
    ids = lax.broadcasted_iota(jnp.int32, values.shape, 0)
    shift = 1
    while shift < rows:
        moved = pltpu.roll(values, shift, 0)
        values = values + jnp.where(ids >= shift, moved, 0.0)
        shift *= 2
    return values


def split_three(values):
    high = values.astype(BF16)
    rest = values - high.astype(F32)
    mid = rest.astype(BF16)
    low = (rest - mid.astype(F32)).astype(BF16)
    return high, mid, low


def projection(head, field_out):
    first = jnp.where(lax.broadcasted_iota(jnp.int32, (1, head.shape[1]), 1) == 0, 1.0, 0.0).astype(BF16)
    density = dot_nn(first, field_out)
    high, mid, low = split_three(head)
    proj = dot_nn(high, field_out) + (dot_nn(mid, field_out) + dot_nn(low, field_out))
    proj_high = proj.astype(BF16).astype(F32)
    rest = proj - proj_high
    eight = jnp.concatenate([density, proj_high, rest, jnp.zeros_like(density)], axis=0)
    return jnp.concatenate([eight, eight], axis=0).astype(BF16)


def positive(values):
    rounded = values.astype(BF16)
    return jnp.maximum(rounded, jnp.zeros_like(rounded))


def where_positive(mask, values):
    rounded = values.astype(BF16)
    return jnp.where(mask > 0, rounded, jnp.zeros_like(rounded))


def forward_kernel(
    x_hbm, spacing_hbm, counts_hbm, first_hbm, last_hbm, direction_hbm, target_hbm,
    w1_hbm, w2_hbm, w3_hbm, head_hbm,
    seg_ref, order_ref, x_ref, h1_ref, h2_ref, save_ref, w16_ref, w2_ref, target_ref,
    w1_ref, w3_ref, head_ref, spacing_ref, counts_ref, first_ref, last_ref, direction_ref, out8, sems,
):
    samples, _, rays = out8.shape
    count = x_ref.shape[0]
    chunk = count // FORWARD_CHUNKS
    moves = [
        pltpu.make_async_copy(source, place, sems.at[i])
        for i, (source, place) in enumerate(
            (
                (head_hbm, head_ref), (w3_hbm, w3_ref), (w1_hbm, w1_ref), (w2_hbm, w2_ref),
                (spacing_hbm, spacing_ref), (counts_hbm, counts_ref), (first_hbm, first_ref),
                (last_hbm, last_ref), (direction_hbm, direction_ref), (target_hbm, target_ref),
            )
        )
    ]
    loads = [
        pltpu.make_async_copy(x_hbm.at[pl.ds(at, size)], x_ref.at[pl.ds(at, size)], sems.at[len(moves) + i])
        for i, (at, size) in enumerate(((0, chunk), (chunk, count - chunk)))
    ]
    for move in moves[2:3] + loads[:1] + moves[3:4] + moves[:2] + loads[1:] + moves[4:]:
        move.start()
    for move in moves[:4] + loads[:1]:
        move.wait()
    w16_ref[...] = projection(head_ref[...], w3_ref[...])

    for c in range(FORWARD_CHUNKS):
        if c == 1:
            for move in moves[4:] + loads[1:]:
                move.wait()
        rows = pl.ds(c * chunk, chunk)
        h1 = positive(dot_nn(x_ref[rows], w1_ref[...]))
        h1_ref[rows] = h1
        h2 = positive(dot_nn(h1, w2_ref[...]))
        h2_ref[rows] = h2
        eight = dot_nt(w16_ref[...], h2)[:8]
        each = chunk // rays
        for j in range(each):
            out8[c * each + j] = eight[:, j * rays : (j + 1) * rays]

    slab = lax.axis_index("slab")
    reverse = jnp.minimum(jnp.maximum(direction_ref[...], 0), 1)
    for bit in range(order_ref.shape[0]):
        higher = (slab >> bit) & 1
        order_ref[bit] = 1 - (reverse ^ higher)
    density = out8[:, 0, :]
    proj = [out8[:, 1 + k, :] + out8[:, 4 + k, :] for k in range(3)]
    ids = lax.broadcasted_iota(jnp.int32, density.shape, 0)
    active = (first_ref[...] <= slab) & (slab < last_ref[...])
    live = jnp.where((ids < counts_ref[...]) & active, 1.0, 0.0)
    span = spacing_ref[...] * live
    optical = (jnp.maximum(density, 0.0) + jnp.log1p(jnp.exp(-jnp.abs(density)))) * span
    running = running_sum(optical)
    column = running[samples - 1 : samples]
    before = jnp.where(direction_ref[...] > 0, column - running, running - optical)
    reach = jnp.exp(-before)
    passed = jnp.exp(-optical)
    weights = reach * (1.0 - passed)
    seg_ref[...] = jnp.concatenate(
        [jnp.exp(-column)] + [jnp.sum(weights * p, axis=0, keepdims=True) for p in proj], axis=0
    )
    save_ref[0] = weights
    save_ref[1] = reach * passed
    save_ref[2] = span * jax.nn.sigmoid(density)
    for k in range(3):
        save_ref[3 + k] = proj[k]


def backward_kernel(
    own_ref, order_ref, h1_ref, h2_ref, save_ref, w16_ref, target_ref, *refs, n_tile,
):
    n_bits = order_ref.shape[0]
    pieces = refs[:n_bits]
    front_hbm, keep_ref, send_ref, back_ref, q16, front_ref, q8, mid_ref, sem = refs[n_bits:]
    samples, _, rays = q8.shape
    count = h1_ref.shape[0]
    slab = lax.axis_index("slab")
    kept = kept_half(lax.axis_index("tile"), n_tile)

    front_trans = back_trans = jnp.ones((1, rays), F32)
    front_color = back_color = jnp.zeros((3, rays), F32)
    for bit in range(n_bits):
        behind = order_ref[bit] > 0
        trans, color = pieces[bit][0:1], pieces[bit][1:4]
        front_color = jnp.where(behind, front_color, color + trans * front_color)
        front_trans = jnp.where(behind, front_trans, trans * front_trans)
        back_color = jnp.where(behind, back_color + back_trans * color, back_color)
        back_trans = jnp.where(behind, back_trans * trans, back_trans)
    forward_ray = (order_ref[0] ^ (slab & 1)) > 0
    front_ref[...] = front_trans
    store = pltpu.make_async_copy(front_ref, front_hbm, sem)
    store.start()
    own = own_ref[...]
    own_trans = own[0:1]
    logits = front_color + front_trans * own[1:4] + (front_trans * own_trans) * back_color
    shade = jax.nn.sigmoid(logits)
    error = (shade - target_ref[...]) / rays
    grad_logit = error * shade * (1.0 - shade)
    grad_trans = front_trans * jnp.sum(grad_logit * back_color, axis=0, keepdims=True)
    pull = front_trans * grad_logit

    weights = save_ref[0]
    grad_weight = pull[0:1] * save_ref[3] + pull[1:2] * save_ref[4] + pull[2:3] * save_ref[5]
    product = weights * grad_weight
    running = running_sum(product)
    total = running[samples - 1 : samples]
    after = jnp.where(forward_ray, total - running, running - product)
    grad_optical = grad_weight * save_ref[1] - after - grad_trans * own_trans
    q8[:, 0, :] = grad_optical * save_ref[2]
    for k in range(3):
        q = weights * pull[k : k + 1]
        q8[:, 1 + k, :] = q
        q8[:, 4 + k, :] = q
    q8[:, 7, :] = jnp.zeros_like(weights)
    for j in range(samples):
        rows = q8[j]
        high = rows.astype(BF16).astype(F32)
        q16[:, j * rays : (j + 1) * rays] = jnp.concatenate([high, rows - high], axis=0).astype(BF16)

    chunk = count // BACKWARD_CHUNKS
    for c in range(BACKWARD_CHUNKS):
        rows = pl.ds(c * chunk, chunk)
        back_two = where_positive(h2_ref[rows], dot_tn(q16[:, rows], w16_ref[...]))
        back_ref[rows] = back_two
        grad_mid = dot_tn(h1_ref[rows], back_two)
        mid_ref[...] = grad_mid if c == 0 else mid_ref[...] + grad_mid

    half = mid_ref.shape[0] // 2
    for place, which in ((send_ref, 1 - kept), (keep_ref, kept)):
        place[...] = mid_ref[pl.ds(pl.multiple_of(which * half, half), half)]
    store.wait()


def inner_kernel(h1_ref, w2_ref, back_ref, one_ref):
    count = h1_ref.shape[0]
    chunk = count // INNER_CHUNKS
    for c in range(INNER_CHUNKS):
        rows = pl.ds(c * chunk, chunk)
        one_ref[rows] = where_positive(h1_ref[rows], dot_nt(back_ref[rows], w2_ref[...]))


def first_kernel(x_ref, one_ref, h2_ref, q16, keep_ref, send_ref, in_ref, out_ref, *, n_tile):
    kept = kept_half(lax.axis_index("tile"), n_tile)
    count = x_ref.shape[0]
    chunk = count // FIRST_CHUNKS
    for c in range(FIRST_CHUNKS):
        rows = pl.ds(c * chunk, chunk)
        grad_in = dot_tn(x_ref[rows], one_ref[rows])
        grad_out = dot_nn(q16[:, rows], h2_ref[rows])
        for ref, part in ((out_ref, grad_out), (in_ref, grad_in)):
            ref[...] = part if c == 0 else ref[...] + part

    half = in_ref.shape[0] // 2
    for place, which in ((send_ref, 1 - kept), (keep_ref, kept)):
        place[:half] = in_ref[pl.ds(pl.multiple_of(which * half, half), half)]
        place[half:] = out_ref[:8] + out_ref[8:]


def expand_kernel(factors_ref, head_ref, out_ref):
    factors = factors_ref[factors_ref.shape[0] - 8 :]
    head = head_ref[...]
    width = head.shape[1]
    first = jnp.where(lax.broadcasted_iota(jnp.int32, (1, width), 1) == 0, 1.0, 0.0)
    rows = jnp.concatenate([first, head, jnp.zeros((4, width), F32)], axis=0)
    out_ref[...] = lax.dot_general(
        rows, factors, (((0,), (0,)), ((), ())), preferred_element_type=F32, precision=lax.Precision.HIGHEST
    )


def final_kernel(own_mid, other_mid, own_in, other_in, out_ref, in_hbm, mid_hbm, out_hbm, sems, *, n_tile):
    kept = kept_half(lax.axis_index("tile"), n_tile)
    half_mid = mid_hbm.shape[0] // 2
    half_in = in_hbm.shape[0] // 2
    moves = []
    for source, place, size, half in (
        (own_mid, mid_hbm, half_mid, kept),
        (other_mid, mid_hbm, half_mid, 1 - kept),
        (own_in, in_hbm, half_in, kept),
        (other_in, in_hbm, half_in, 1 - kept),
    ):
        moves.append(
            pltpu.make_async_copy(
                source.at[pl.ds(0, size)],
                place.at[pl.ds(pl.multiple_of(half * size, size), size)],
                sems.at[len(moves)],
            )
        )
    moves.append(pltpu.make_async_copy(out_ref, out_hbm, sems.at[len(moves)]))
    for move in moves:
        move.start()
    for move in moves:
        move.wait()


def kept_half(tile, n_tile):
    half = tile & 1
    shift = 1
    while (1 << shift) < n_tile:
        half = half ^ ((tile >> shift) & 1)
        shift += 1
    return half


def joined(own, got, own_first):
    first = jnp.where(own_first, own, got)
    second = jnp.where(own_first, got, own)
    row = lax.broadcasted_iota(jnp.int32, own.shape, 0)
    return first[0:1] * second + jnp.where(row == 0, 0.0, first)


def pairs(size, bit):
    return [(i, i ^ bit) for i in range(size)]


def make_body(n_slab, n_tile):

    def body(
        encoded, spacing, counts, seg_first, seg_last, direction,
        field_in, field_mid, field_out, color_head, target,
    ):
        _, samples, rays, width = encoded.shape
        hidden = field_mid.shape[1]
        features = field_out.shape[2]
        count = samples * rays
        n_bits = (n_slab - 1).bit_length()
        row = lambda a: a.reshape(1, rays)
        seg, order, *kept = pl.pallas_call(
            forward_kernel,
            name="forward",
            out_shape=(
                pltpu.VMEM((4, rays), F32),
                pltpu.VMEM((n_bits, 1, rays), jnp.int32),
                pltpu.VMEM((count, width), BF16),
                pltpu.VMEM((count, hidden), BF16),
                pltpu.VMEM((count, hidden), BF16),
                pltpu.VMEM((6, samples, rays), F32),
                pltpu.VMEM((16, hidden), BF16),
                pltpu.VMEM((hidden, hidden), BF16),
                pltpu.VMEM((3, rays), F32),
            ),
            in_specs=[HBM] * 11,
            out_specs=(VMEM,) * 9,
            scratch_shapes=[
                pltpu.VMEM((width, hidden), BF16),
                pltpu.VMEM((features, hidden), BF16),
                pltpu.VMEM((3, features), F32),
                pltpu.VMEM((samples, rays), F32),
                pltpu.VMEM((1, rays), jnp.int32),
                pltpu.VMEM((1, rays), jnp.int32),
                pltpu.VMEM((1, rays), jnp.int32),
                pltpu.VMEM((1, rays), jnp.int32),
                pltpu.VMEM((samples, 8, rays), F32),
                pltpu.SemaphoreType.DMA((12,)),
            ],
            compiler_params=LIMIT,
        )(
            *(
                pltpu.with_memory_space_constraint(a, pltpu.HBM)
                for a in (
                    encoded[0].reshape(count, width), spacing[0], counts, row(seg_first), row(seg_last),
                    row(direction), target.T, field_in[0], field_mid[0], field_out[0].T, color_head.T,
                )
            ),
        )

        block = seg
        pieces = []
        for bit in range(n_bits):
            got = lax.ppermute(block, "slab", pairs(n_slab, 1 << bit))
            pieces.append(got)
            if bit + 1 < n_bits:
                block = joined(block, got, order[bit] > 0)

        x, h1, h2, save, w16, w2, target_rows = kept
        half_mid, half_in = hidden // 2, width // 2 + 8
        front, keep_mid, send_mid, back, factors = pl.pallas_call(
            functools.partial(backward_kernel, n_tile=n_tile),
            name="backward",
            out_shape=(
                pltpu.HBM((1, rays), F32),
                pltpu.VMEM((half_mid, hidden), F32),
                pltpu.VMEM((half_mid, hidden), F32),
                pltpu.VMEM((count, hidden), BF16),
                pltpu.VMEM((16, count), BF16),
            ),
            in_specs=[VMEM] * (7 + n_bits),
            out_specs=(HBM, VMEM, VMEM, VMEM, VMEM),
            scratch_shapes=[
                pltpu.VMEM((1, rays), F32),
                pltpu.VMEM((samples, 8, rays), F32),
                pltpu.VMEM((hidden, hidden), F32),
                pltpu.SemaphoreType.DMA,
            ],
            compiler_params=LIMIT,
            cost_estimate=pl.CostEstimate(flops=4 * count * hidden * hidden, bytes_accessed=0, transcendentals=0),
        )(seg, order, h1, h2, save, w16, target_rows, *pieces)
        back_one = pl.pallas_call(
            inner_kernel,
            name="inner",
            out_shape=pltpu.VMEM((count, hidden), BF16),
            in_specs=[VMEM] * 3,
            out_specs=VMEM,
            compiler_params=LIMIT,
            cost_estimate=pl.CostEstimate(flops=2 * count * hidden * hidden, bytes_accessed=0, transcendentals=0),
        )(h1, w2, back)

        def chip_sum(keep, send):
            return keep + lax.ppermute(send, "tile", pairs(n_tile, 1))

        def tile_sum(part):
            bit = 2
            while bit < n_tile:
                part = part + lax.ppermute(part, "tile", pairs(n_tile, bit | 1))
                bit *= 2
            return part, lax.ppermute(part, "tile", pairs(n_tile, 1))

        part_mid = chip_sum(keep_mid, send_mid)
        keep_in, send_in = pl.pallas_call(
            functools.partial(first_kernel, n_tile=n_tile),
            name="first",
            out_shape=(pltpu.VMEM((half_in, hidden), F32), pltpu.VMEM((half_in, hidden), F32)),
            in_specs=[VMEM] * 4,
            out_specs=(VMEM, VMEM),
            scratch_shapes=[pltpu.VMEM((width, hidden), F32), pltpu.VMEM((16, hidden), F32)],
            compiler_params=LIMIT,
            cost_estimate=pl.CostEstimate(flops=4 * count * hidden * hidden, bytes_accessed=0, transcendentals=0),
        )(x, back_one, h2, factors)

        part_mid, keep_in, send_in = lax.optimization_barrier((part_mid, keep_in, send_in))
        own_mid, other_mid = tile_sum(part_mid)
        own_in, other_in = tile_sum(chip_sum(keep_in, send_in))
        expanded = pl.pallas_call(
            expand_kernel,
            name="expand",
            out_shape=pltpu.VMEM((features, hidden), F32),
            in_specs=[VMEM] * 2,
            out_specs=VMEM,
            compiler_params=LIMIT,
            cost_estimate=pl.CostEstimate(flops=2 * 8 * features * hidden * 6, bytes_accessed=0, transcendentals=0),
        )(own_in, color_head.T)
        grad_in, grad_mid, grad_out = pl.pallas_call(
            functools.partial(final_kernel, n_tile=n_tile),
            name="final",
            out_shape=(
                pltpu.HBM((width, hidden), F32),
                pltpu.HBM((hidden, hidden), F32),
                pltpu.HBM((features, hidden), F32),
            ),
            in_specs=[VMEM] * 5,
            out_specs=(HBM,) * 3,
            scratch_shapes=[pltpu.SemaphoreType.DMA((5,))],
            compiler_params=LIMIT,
        )(own_mid, other_mid, own_in, other_in, expanded)
        return front, grad_in[None], grad_mid[None], grad_out.T[None]

    return body


def solution(mesh):
    return jax.shard_map(
        make_body(mesh.shape["slab"], mesh.shape["tile"]),
        mesh=mesh,
        in_specs=(
            P("slab", None, "tile", None),
            P("slab", None, "tile"),
            P("slab", "tile"),
            P("tile"),
            P("tile"),
            P("tile"),
            P("slab", None, None),
            P("slab", None, None),
            P("slab", None, None),
            P(),
            P("tile", None),
        ),
        out_specs=(
            P("slab", "tile"),
            P("slab", None, None),
            P("slab", None, None),
            P("slab", None, None),
        ),
        check_vma=False,
    )
```

```python
import functools

import jax
import jax.numpy as jnp
from jax import lax
from jax.experimental import pallas as pl
from jax.experimental.pallas import tpu as pltpu
from jax.sharding import PartitionSpec as P

F32 = jnp.float32
BF16 = jnp.bfloat16
VMEM = pl.BlockSpec(memory_space=pltpu.VMEM)
HBM = pl.BlockSpec(memory_space=pltpu.HBM)
LIMIT = pltpu.CompilerParams(vmem_limit_bytes=32 * 1024 * 1024)
FIRST_LOAD = 4
BACKWARD_CHUNKS = 8
FIRST_CHUNKS = 8


def dot_nn(a, b):
    return lax.dot_general(a, b, (((1,), (0,)), ((), ())), preferred_element_type=F32)


def dot_nt(a, b):
    return lax.dot_general(a, b, (((1,), (1,)), ((), ())), preferred_element_type=F32)


def dot_tn(a, b):
    return lax.dot_general(a, b, (((0,), (0,)), ((), ())), preferred_element_type=F32)


def running_sum(values):
    rows = values.shape[0]
    ids = lax.broadcasted_iota(jnp.int32, values.shape, 0)
    shift = 1
    while shift < rows:
        moved = pltpu.roll(values, shift, 0)
        values = values + jnp.where(ids >= shift, moved, 0.0)
        shift *= 2
    return values


def split_three(values):
    high = values.astype(BF16)
    rest = values - high.astype(F32)
    mid = rest.astype(BF16)
    low = (rest - mid.astype(F32)).astype(BF16)
    return high, mid, low


def projection(head, field_out):
    first = jnp.where(lax.broadcasted_iota(jnp.int32, (1, head.shape[1]), 1) == 0, 1.0, 0.0).astype(BF16)
    density = dot_nn(first, field_out)
    high, mid, low = split_three(head)
    proj = dot_nn(high, field_out) + (dot_nn(mid, field_out) + dot_nn(low, field_out))
    proj_high = proj.astype(BF16).astype(F32)
    rest = proj - proj_high
    eight = jnp.concatenate([density, proj_high, rest, jnp.zeros_like(density)], axis=0)
    return jnp.concatenate([eight, eight], axis=0).astype(BF16)


def positive(values):
    rounded = values.astype(BF16)
    return jnp.maximum(rounded, jnp.zeros_like(rounded))


def where_positive(mask, values):
    rounded = values.astype(BF16)
    return jnp.where(mask > 0, rounded, jnp.zeros_like(rounded))


def forward_kernel(
    x_hbm, spacing_hbm, counts_hbm, first_hbm, last_hbm, direction_hbm, target_hbm,
    w1_hbm, w2_hbm, w3_hbm, head_hbm,
    seg_ref, order_ref, x_ref, h1_ref, h2_ref, save_ref, w16_ref, w2_ref, target_ref,
    w1_ref, w3_ref, head_ref, spacing_ref, counts_ref, first_ref, last_ref, direction_ref, out8, sems,
):
    samples, _, rays = out8.shape
    count = x_ref.shape[0]
    first_rows = min(FIRST_LOAD, samples) * rays
    moves = [
        pltpu.make_async_copy(source, place, sems.at[i])
        for i, (source, place) in enumerate(
            (
                (head_hbm, head_ref), (w3_hbm, w3_ref), (w1_hbm, w1_ref), (w2_hbm, w2_ref),
                (spacing_hbm, spacing_ref), (counts_hbm, counts_ref), (first_hbm, first_ref),
                (last_hbm, last_ref), (direction_hbm, direction_ref), (target_hbm, target_ref),
            )
        )
    ]
    loads = [
        pltpu.make_async_copy(x_hbm.at[pl.ds(at, size)], x_ref.at[pl.ds(at, size)], sems.at[len(moves) + i])
        for i, (at, size) in enumerate(((0, first_rows), (first_rows, count - first_rows)))
    ]
    for move in moves[2:3] + loads[:1] + moves[3:4] + moves[:2] + loads[1:] + moves[4:]:
        move.start()
    for move in moves[:4] + loads[:1]:
        move.wait()
    w16_ref[...] = projection(head_ref[...], w3_ref[...])

    for c in range(samples + 2):
        if c == first_rows // rays:
            for move in moves[4:] + loads[1:]:
                move.wait()
        if c < samples:
            rows = pl.ds(c * rays, rays)
            h1_ref[rows] = positive(dot_nn(x_ref[rows], w1_ref[...]))
        if 0 <= c - 1 < samples:
            rows = pl.ds((c - 1) * rays, rays)
            h2_ref[rows] = positive(dot_nn(h1_ref[rows], w2_ref[...]))
        if 0 <= c - 2 < samples:
            out8[c - 2] = dot_nt(w16_ref[...], h2_ref[pl.ds((c - 2) * rays, rays)])[:8]

    slab = lax.axis_index("slab")
    reverse = jnp.minimum(jnp.maximum(direction_ref[...], 0), 1)
    for bit in range(order_ref.shape[0]):
        higher = (slab >> bit) & 1
        order_ref[bit] = 1 - (reverse ^ higher)
    density = out8[:, 0, :]
    proj = [out8[:, 1 + k, :] + out8[:, 4 + k, :] for k in range(3)]
    ids = lax.broadcasted_iota(jnp.int32, density.shape, 0)
    active = (first_ref[...] <= slab) & (slab < last_ref[...])
    live = jnp.where((ids < counts_ref[...]) & active, 1.0, 0.0)
    span = spacing_ref[...] * live
    optical = (jnp.maximum(density, 0.0) + jnp.log1p(jnp.exp(-jnp.abs(density)))) * span
    running = running_sum(optical)
    column = running[samples - 1 : samples]
    before = jnp.where(direction_ref[...] > 0, column - running, running - optical)
    reach = jnp.exp(-before)
    passed = jnp.exp(-optical)
    weights = reach * (1.0 - passed)
    seg_ref[...] = jnp.concatenate(
        [jnp.exp(-column)] + [jnp.sum(weights * p, axis=0, keepdims=True) for p in proj], axis=0
    )
    save_ref[0] = weights
    save_ref[1] = reach * passed
    save_ref[2] = span * jax.nn.sigmoid(density)
    for k in range(3):
        save_ref[3 + k] = proj[k]


def backward_kernel(
    own_ref, order_ref, h1_ref, h2_ref, save_ref, w16_ref, w2_ref, target_ref, *refs, n_tile,
):
    n_bits = order_ref.shape[0]
    pieces = refs[:n_bits]
    front_hbm, keep_ref, send_ref, one_ref, q16, front_ref, q8, mid_ref, sem = refs[n_bits:]
    samples, _, rays = q8.shape
    count = h1_ref.shape[0]
    slab = lax.axis_index("slab")
    kept = kept_half(lax.axis_index("tile"), n_tile)

    front_trans = back_trans = jnp.ones((1, rays), F32)
    front_color = back_color = jnp.zeros((3, rays), F32)
    for bit in range(n_bits):
        behind = order_ref[bit] > 0
        trans, color = pieces[bit][0:1], pieces[bit][1:4]
        front_color = jnp.where(behind, front_color, color + trans * front_color)
        front_trans = jnp.where(behind, front_trans, trans * front_trans)
        back_color = jnp.where(behind, back_color + back_trans * color, back_color)
        back_trans = jnp.where(behind, back_trans * trans, back_trans)
    forward_ray = (order_ref[0] ^ (slab & 1)) > 0
    front_ref[...] = front_trans
    store = pltpu.make_async_copy(front_ref, front_hbm, sem)
    store.start()
    own = own_ref[...]
    own_trans = own[0:1]
    logits = front_color + front_trans * own[1:4] + (front_trans * own_trans) * back_color
    shade = jax.nn.sigmoid(logits)
    error = (shade - target_ref[...]) / rays
    grad_logit = error * shade * (1.0 - shade)
    grad_trans = front_trans * jnp.sum(grad_logit * back_color, axis=0, keepdims=True)
    pull = front_trans * grad_logit

    weights = save_ref[0]
    grad_weight = pull[0:1] * save_ref[3] + pull[1:2] * save_ref[4] + pull[2:3] * save_ref[5]
    product = weights * grad_weight
    running = running_sum(product)
    total = running[samples - 1 : samples]
    after = jnp.where(forward_ray, total - running, running - product)
    grad_optical = grad_weight * save_ref[1] - after - grad_trans * own_trans
    q8[:, 0, :] = grad_optical * save_ref[2]
    for k in range(3):
        q = weights * pull[k : k + 1]
        q8[:, 1 + k, :] = q
        q8[:, 4 + k, :] = q
    q8[:, 7, :] = jnp.zeros_like(weights)
    for j in range(samples):
        rows = q8[j]
        high = rows.astype(BF16).astype(F32)
        q16[:, j * rays : (j + 1) * rays] = jnp.concatenate([high, rows - high], axis=0).astype(BF16)

    chunk = count // BACKWARD_CHUNKS
    def back_two(c):
        rows = pl.ds(c * chunk, chunk)
        return where_positive(h2_ref[rows], dot_tn(q16[:, rows], w16_ref[...]))

    later = back_two(0)
    for c in range(BACKWARD_CHUNKS):
        rows = pl.ds(c * chunk, chunk)
        now = later
        if c + 1 < BACKWARD_CHUNKS:
            later = back_two(c + 1)
        grad_mid = dot_tn(h1_ref[rows], now)
        mid_ref[...] = grad_mid if c == 0 else mid_ref[...] + grad_mid
        one_ref[rows] = where_positive(h1_ref[rows], dot_nt(now, w2_ref[...]))

    half = mid_ref.shape[0] // 2
    for place, which in ((send_ref, 1 - kept), (keep_ref, kept)):
        place[...] = mid_ref[pl.ds(pl.multiple_of(which * half, half), half)]
    store.wait()


def first_kernel(x_ref, one_ref, h2_ref, q16, keep_ref, send_ref, in_ref, out_ref, *, n_tile):
    kept = kept_half(lax.axis_index("tile"), n_tile)
    count = x_ref.shape[0]
    chunk = count // FIRST_CHUNKS
    for c in range(FIRST_CHUNKS):
        rows = pl.ds(c * chunk, chunk)
        grad_in = dot_tn(x_ref[rows], one_ref[rows])
        grad_out = dot_nn(q16[:, rows], h2_ref[rows])
        for ref, part in ((out_ref, grad_out), (in_ref, grad_in)):
            ref[...] = part if c == 0 else ref[...] + part

    half = in_ref.shape[0] // 2
    for place, which in ((send_ref, 1 - kept), (keep_ref, kept)):
        place[:half] = in_ref[pl.ds(pl.multiple_of(which * half, half), half)]
        place[half:] = out_ref[:8] + out_ref[8:]


def expand_kernel(factors_ref, head_ref, out_ref):
    factors = factors_ref[factors_ref.shape[0] - 8 :]
    head = head_ref[...]
    width = head.shape[1]
    first = jnp.where(lax.broadcasted_iota(jnp.int32, (1, width), 1) == 0, 1.0, 0.0)
    rows = jnp.concatenate([first, head, jnp.zeros((4, width), F32)], axis=0)
    out_ref[...] = lax.dot_general(
        rows, factors, (((0,), (0,)), ((), ())), preferred_element_type=F32, precision=lax.Precision.HIGHEST
    )


def final_kernel(own_mid, other_mid, own_in, other_in, out_ref, in_hbm, mid_hbm, out_hbm, sems, *, n_tile):
    kept = kept_half(lax.axis_index("tile"), n_tile)
    half_mid = mid_hbm.shape[0] // 2
    half_in = in_hbm.shape[0] // 2
    moves = []
    for source, place, size, half in (
        (own_mid, mid_hbm, half_mid, kept),
        (other_mid, mid_hbm, half_mid, 1 - kept),
        (own_in, in_hbm, half_in, kept),
        (other_in, in_hbm, half_in, 1 - kept),
    ):
        moves.append(
            pltpu.make_async_copy(
                source.at[pl.ds(0, size)],
                place.at[pl.ds(pl.multiple_of(half * size, size), size)],
                sems.at[len(moves)],
            )
        )
    moves.append(pltpu.make_async_copy(out_ref, out_hbm, sems.at[len(moves)]))
    for move in moves:
        move.start()
    for move in moves:
        move.wait()


def kept_half(tile, n_tile):
    half = tile & 1
    shift = 1
    while (1 << shift) < n_tile:
        half = half ^ ((tile >> shift) & 1)
        shift += 1
    return half


def joined(own, got, own_first):
    first = jnp.where(own_first, own, got)
    second = jnp.where(own_first, got, own)
    row = lax.broadcasted_iota(jnp.int32, own.shape, 0)
    return first[0:1] * second + jnp.where(row == 0, 0.0, first)


def pairs(size, bit):
    return [(i, i ^ bit) for i in range(size)]


def make_body(n_slab, n_tile):

    def body(
        encoded, spacing, counts, seg_first, seg_last, direction,
        field_in, field_mid, field_out, color_head, target,
    ):
        _, samples, rays, width = encoded.shape
        hidden = field_mid.shape[1]
        features = field_out.shape[2]
        count = samples * rays
        n_bits = (n_slab - 1).bit_length()
        row = lambda a: a.reshape(1, rays)
        seg, order, *kept = pl.pallas_call(
            forward_kernel,
            name="forward",
            out_shape=(
                pltpu.VMEM((4, rays), F32),
                pltpu.VMEM((n_bits, 1, rays), jnp.int32),
                pltpu.VMEM((count, width), BF16),
                pltpu.VMEM((count, hidden), BF16),
                pltpu.VMEM((count, hidden), BF16),
                pltpu.VMEM((6, samples, rays), F32),
                pltpu.VMEM((16, hidden), BF16),
                pltpu.VMEM((hidden, hidden), BF16),
                pltpu.VMEM((3, rays), F32),
            ),
            in_specs=[HBM] * 11,
            out_specs=(VMEM,) * 9,
            scratch_shapes=[
                pltpu.VMEM((width, hidden), BF16),
                pltpu.VMEM((features, hidden), BF16),
                pltpu.VMEM((3, features), F32),
                pltpu.VMEM((samples, rays), F32),
                pltpu.VMEM((1, rays), jnp.int32),
                pltpu.VMEM((1, rays), jnp.int32),
                pltpu.VMEM((1, rays), jnp.int32),
                pltpu.VMEM((1, rays), jnp.int32),
                pltpu.VMEM((samples, 8, rays), F32),
                pltpu.SemaphoreType.DMA((12,)),
            ],
            compiler_params=LIMIT,
        )(
            *(
                pltpu.with_memory_space_constraint(a, pltpu.HBM)
                for a in (
                    encoded[0].reshape(count, width), spacing[0], counts, row(seg_first), row(seg_last),
                    row(direction), target.T, field_in[0], field_mid[0], field_out[0].T, color_head.T,
                )
            ),
        )

        block = seg
        pieces = []
        for bit in range(n_bits):
            got = lax.ppermute(block, "slab", pairs(n_slab, 1 << bit))
            pieces.append(got)
            if bit + 1 < n_bits:
                block = joined(block, got, order[bit] > 0)

        x, h1, h2, save, w16, w2, target_rows = kept
        half_mid, half_in = hidden // 2, width // 2 + 8
        front, keep_mid, send_mid, back_one, factors = pl.pallas_call(
            functools.partial(backward_kernel, n_tile=n_tile),
            name="backward",
            out_shape=(
                pltpu.HBM((1, rays), F32),
                pltpu.VMEM((half_mid, hidden), F32),
                pltpu.VMEM((half_mid, hidden), F32),
                pltpu.VMEM((count, hidden), BF16),
                pltpu.VMEM((16, count), BF16),
            ),
            in_specs=[VMEM] * (8 + n_bits),
            out_specs=(HBM, VMEM, VMEM, VMEM, VMEM),
            scratch_shapes=[
                pltpu.VMEM((1, rays), F32),
                pltpu.VMEM((samples, 8, rays), F32),
                pltpu.VMEM((hidden, hidden), F32),
                pltpu.SemaphoreType.DMA,
            ],
            compiler_params=LIMIT,
            cost_estimate=pl.CostEstimate(flops=4 * count * hidden * hidden, bytes_accessed=0, transcendentals=0),
        )(seg, order, h1, h2, save, w16, w2, target_rows, *pieces)
        def chip_sum(keep, send):
            return keep + lax.ppermute(send, "tile", pairs(n_tile, 1))

        def tile_sum(part):
            bit = 2
            while bit < n_tile:
                part = part + lax.ppermute(part, "tile", pairs(n_tile, bit | 1))
                bit *= 2
            return part, lax.ppermute(part, "tile", pairs(n_tile, 1))

        part_mid = chip_sum(keep_mid, send_mid)
        keep_in, send_in = pl.pallas_call(
            functools.partial(first_kernel, n_tile=n_tile),
            name="first",
            out_shape=(pltpu.VMEM((half_in, hidden), F32), pltpu.VMEM((half_in, hidden), F32)),
            in_specs=[VMEM] * 4,
            out_specs=(VMEM, VMEM),
            scratch_shapes=[pltpu.VMEM((width, hidden), F32), pltpu.VMEM((16, hidden), F32)],
            compiler_params=LIMIT,
            cost_estimate=pl.CostEstimate(flops=4 * count * hidden * hidden, bytes_accessed=0, transcendentals=0),
        )(x, back_one, h2, factors)

        part_mid, keep_in, send_in = lax.optimization_barrier((part_mid, keep_in, send_in))
        own_mid, other_mid = tile_sum(part_mid)
        own_in, other_in = tile_sum(chip_sum(keep_in, send_in))
        expanded = pl.pallas_call(
            expand_kernel,
            name="expand",
            out_shape=pltpu.VMEM((features, hidden), F32),
            in_specs=[VMEM] * 2,
            out_specs=VMEM,
            compiler_params=LIMIT,
            cost_estimate=pl.CostEstimate(flops=2 * 8 * features * hidden * 6, bytes_accessed=0, transcendentals=0),
        )(own_in, color_head.T)
        grad_in, grad_mid, grad_out = pl.pallas_call(
            functools.partial(final_kernel, n_tile=n_tile),
            name="final",
            out_shape=(
                pltpu.HBM((width, hidden), F32),
                pltpu.HBM((hidden, hidden), F32),
                pltpu.HBM((features, hidden), F32),
            ),
            in_specs=[VMEM] * 5,
            out_specs=(HBM,) * 3,
            scratch_shapes=[pltpu.SemaphoreType.DMA((5,))],
            compiler_params=LIMIT,
        )(own_mid, other_mid, own_in, other_in, expanded)
        return front, grad_in[None], grad_mid[None], grad_out.T[None]

    return body


def solution(mesh):
    return jax.shard_map(
        make_body(mesh.shape["slab"], mesh.shape["tile"]),
        mesh=mesh,
        in_specs=(
            P("slab", None, "tile", None),
            P("slab", None, "tile"),
            P("slab", "tile"),
            P("tile"),
            P("tile"),
            P("tile"),
            P("slab", None, None),
            P("slab", None, None),
            P("slab", None, None),
            P(),
            P("tile", None),
        ),
        out_specs=(
            P("slab", "tile"),
            P("slab", None, None),
            P("slab", None, None),
            P("slab", None, None),
        ),
        check_vma=False,
    )
```

```python
import functools

import jax
import jax.numpy as jnp
from jax import lax
from jax.experimental import pallas as pl
from jax.experimental.pallas import tpu as pltpu
from jax.sharding import PartitionSpec as P

F32 = jnp.float32
BF16 = jnp.bfloat16
VMEM = pl.BlockSpec(memory_space=pltpu.VMEM)
HBM = pl.BlockSpec(memory_space=pltpu.HBM)
LIMIT = pltpu.CompilerParams(vmem_limit_bytes=32 * 1024 * 1024)
FIRST_LOAD = 4
BACKWARD_CHUNKS = 8
FIRST_CHUNKS = 8


def dot_nn(a, b):
    return lax.dot_general(a, b, (((1,), (0,)), ((), ())), preferred_element_type=F32)


def dot_nt(a, b):
    return lax.dot_general(a, b, (((1,), (1,)), ((), ())), preferred_element_type=F32)


def dot_tn(a, b):
    return lax.dot_general(a, b, (((0,), (0,)), ((), ())), preferred_element_type=F32)


def running_sum(values):
    rows = values.shape[0]
    ids = lax.broadcasted_iota(jnp.int32, values.shape, 0)
    shift = 1
    while shift < rows:
        moved = pltpu.roll(values, shift, 0)
        values = values + jnp.where(ids >= shift, moved, 0.0)
        shift *= 2
    return values


def split_three(values):
    high = values.astype(BF16)
    rest = values - high.astype(F32)
    mid = rest.astype(BF16)
    low = (rest - mid.astype(F32)).astype(BF16)
    return high, mid, low


def projection(head, field_out):
    first = jnp.where(lax.broadcasted_iota(jnp.int32, (1, head.shape[1]), 1) == 0, 1.0, 0.0).astype(BF16)
    density = dot_nn(first, field_out)
    high, mid, low = split_three(head)
    proj = dot_nn(high, field_out) + (dot_nn(mid, field_out) + dot_nn(low, field_out))
    proj_high = proj.astype(BF16).astype(F32)
    rest = proj - proj_high
    eight = jnp.concatenate([density, proj_high, rest, jnp.zeros_like(density)], axis=0)
    return jnp.concatenate([eight, eight], axis=0).astype(BF16)


def positive(values):
    rounded = values.astype(BF16)
    return jnp.maximum(rounded, jnp.zeros_like(rounded))


def where_positive(mask, values):
    rounded = values.astype(BF16)
    return jnp.where(mask > 0, rounded, jnp.zeros_like(rounded))


def forward_kernel(
    x_hbm, spacing_hbm, counts_hbm, first_hbm, last_hbm, direction_hbm, target_hbm,
    w1_hbm, w2_hbm, w3_hbm, head_hbm,
    seg_ref, x_ref, h1_ref, h2_ref, save_ref, w16_ref, w2_ref, target_ref,
    w1_ref, w3_ref, head_ref, spacing_ref, counts_ref, first_ref, last_ref, direction_ref, out8, sems, *, n_bits,
):
    samples, _, rays = out8.shape
    count = x_ref.shape[0]
    first_rows = min(FIRST_LOAD, samples) * rays
    moves = [
        pltpu.make_async_copy(source, place, sems.at[i])
        for i, (source, place) in enumerate(
            (
                (head_hbm, head_ref), (w3_hbm, w3_ref), (w1_hbm, w1_ref), (w2_hbm, w2_ref),
                (spacing_hbm, spacing_ref), (counts_hbm, counts_ref), (first_hbm, first_ref),
                (last_hbm, last_ref), (direction_hbm, direction_ref), (target_hbm, target_ref),
            )
        )
    ]
    loads = [
        pltpu.make_async_copy(x_hbm.at[pl.ds(at, size)], x_ref.at[pl.ds(at, size)], sems.at[len(moves) + i])
        for i, (at, size) in enumerate(((0, first_rows), (first_rows, count - first_rows)))
    ]
    for move in moves[2:3] + loads[:1] + moves[3:4] + moves[:2] + loads[1:] + moves[4:]:
        move.start()
    for move in moves[:4] + loads[:1]:
        move.wait()
    w16_ref[...] = projection(head_ref[...], w3_ref[...])

    for c in range(samples + 2):
        if c == first_rows // rays:
            for move in moves[4:] + loads[1:]:
                move.wait()
        if c < samples:
            rows = pl.ds(c * rays, rays)
            h1_ref[rows] = positive(dot_nn(x_ref[rows], w1_ref[...]))
        if 0 <= c - 1 < samples:
            rows = pl.ds((c - 1) * rays, rays)
            h2_ref[rows] = positive(dot_nn(h1_ref[rows], w2_ref[...]))
        if 0 <= c - 2 < samples:
            out8[c - 2] = dot_nt(w16_ref[...], h2_ref[pl.ds((c - 2) * rays, rays)])[:8]

    slab = lax.axis_index("slab")
    reverse = jnp.minimum(jnp.maximum(direction_ref[...], 0), 1)
    ahead = [(1 - (reverse ^ ((slab >> bit) & 1))).astype(F32) for bit in range(n_bits)]
    ahead += [jnp.zeros_like(ahead[0])] * (seg_ref.shape[0] - 4 - n_bits)
    density = out8[:, 0, :]
    proj = [out8[:, 1 + k, :] + out8[:, 4 + k, :] for k in range(3)]
    ids = lax.broadcasted_iota(jnp.int32, density.shape, 0)
    active = (first_ref[...] <= slab) & (slab < last_ref[...])
    live = jnp.where((ids < counts_ref[...]) & active, 1.0, 0.0)
    span = spacing_ref[...] * live
    optical = (jnp.maximum(density, 0.0) + jnp.log1p(jnp.exp(-jnp.abs(density)))) * span
    running = running_sum(optical)
    column = running[samples - 1 : samples]
    before = jnp.where(direction_ref[...] > 0, column - running, running - optical)
    reach = jnp.exp(-before)
    passed = jnp.exp(-optical)
    weights = reach * (1.0 - passed)
    seg_ref[...] = jnp.concatenate(
        [jnp.exp(-column)] + [jnp.sum(weights * p, axis=0, keepdims=True) for p in proj] + ahead, axis=0
    )
    save_ref[0] = weights
    save_ref[1] = reach * passed
    save_ref[2] = span * jax.nn.sigmoid(density)
    for k in range(3):
        save_ref[3 + k] = proj[k]


def backward_kernel(
    own_ref, h1_ref, h2_ref, save_ref, w16_ref, w2_ref, target_ref, *refs, n_bits, n_tile,
):
    pieces = refs[:n_bits]
    front_hbm, keep_ref, send_ref, one_ref, q16, front_ref, q8, mid_ref, sem = refs[n_bits:]
    samples, _, rays = q8.shape
    count = h1_ref.shape[0]
    slab = lax.axis_index("slab")
    kept = kept_half(lax.axis_index("tile"), n_tile)

    front_trans = back_trans = jnp.ones((1, rays), F32)
    front_color = back_color = jnp.zeros((3, rays), F32)
    for bit in range(n_bits):
        behind = own_ref[4 + bit : 5 + bit] > 0
        trans, color = pieces[bit][1, 0:1], pieces[bit][1, 1:4]
        front_color = jnp.where(behind, front_color, color + trans * front_color)
        front_trans = jnp.where(behind, front_trans, trans * front_trans)
        back_color = jnp.where(behind, back_color + back_trans * color, back_color)
        back_trans = jnp.where(behind, back_trans * trans, back_trans)
    forward_ray = own_ref[4:5] + (slab & 1).astype(F32) == 1.0
    front_ref[...] = front_trans
    store = pltpu.make_async_copy(front_ref, front_hbm, sem)
    store.start()
    own = own_ref[...]
    own_trans = own[0:1]
    logits = front_color + front_trans * own[1:4] + (front_trans * own_trans) * back_color
    shade = jax.nn.sigmoid(logits)
    error = (shade - target_ref[...]) / rays
    grad_logit = error * shade * (1.0 - shade)
    grad_trans = front_trans * jnp.sum(grad_logit * back_color, axis=0, keepdims=True)
    pull = front_trans * grad_logit

    weights = save_ref[0]
    grad_weight = pull[0:1] * save_ref[3] + pull[1:2] * save_ref[4] + pull[2:3] * save_ref[5]
    product = weights * grad_weight
    running = running_sum(product)
    total = running[samples - 1 : samples]
    after = jnp.where(forward_ray, total - running, running - product)
    grad_optical = grad_weight * save_ref[1] - after - grad_trans * own_trans
    q8[:, 0, :] = grad_optical * save_ref[2]
    for k in range(3):
        q = weights * pull[k : k + 1]
        q8[:, 1 + k, :] = q
        q8[:, 4 + k, :] = q
    q8[:, 7, :] = jnp.zeros_like(weights)
    for j in range(samples):
        rows = q8[j]
        high = rows.astype(BF16).astype(F32)
        q16[:, j * rays : (j + 1) * rays] = jnp.concatenate([high, rows - high], axis=0).astype(BF16)

    chunk = count // BACKWARD_CHUNKS
    def back_two(c):
        rows = pl.ds(c * chunk, chunk)
        return where_positive(h2_ref[rows], dot_tn(q16[:, rows], w16_ref[...]))

    later = back_two(0)
    for c in range(BACKWARD_CHUNKS):
        rows = pl.ds(c * chunk, chunk)
        now = later
        if c + 1 < BACKWARD_CHUNKS:
            later = back_two(c + 1)
        grad_mid = dot_tn(h1_ref[rows], now)
        mid_ref[...] = grad_mid if c == 0 else mid_ref[...] + grad_mid
        one_ref[rows] = where_positive(h1_ref[rows], dot_nt(now, w2_ref[...]))

    half = mid_ref.shape[0] // 2
    for place, which in ((send_ref, 1 - kept), (keep_ref, kept)):
        place[...] = mid_ref[pl.ds(pl.multiple_of(which * half, half), half)]
    store.wait()


def first_kernel(x_ref, one_ref, h2_ref, q16, keep_ref, send_ref, in_ref, out_ref, *, n_tile):
    kept = kept_half(lax.axis_index("tile"), n_tile)
    count = x_ref.shape[0]
    chunk = count // FIRST_CHUNKS
    for c in range(FIRST_CHUNKS):
        rows = pl.ds(c * chunk, chunk)
        grad_in = dot_tn(x_ref[rows], one_ref[rows])
        grad_out = dot_nn(q16[:, rows], h2_ref[rows])
        for ref, part in ((out_ref, grad_out), (in_ref, grad_in)):
            ref[...] = part if c == 0 else ref[...] + part

    half = in_ref.shape[0] // 2
    for place, which in ((send_ref, 1 - kept), (keep_ref, kept)):
        place[:half] = in_ref[pl.ds(pl.multiple_of(which * half, half), half)]
        place[half:] = out_ref[:8] + out_ref[8:]


def expand_kernel(factors_ref, head_ref, out_ref):
    factors = factors_ref[factors_ref.shape[0] - 8 :]
    head = head_ref[...]
    width = head.shape[1]
    first = jnp.where(lax.broadcasted_iota(jnp.int32, (1, width), 1) == 0, 1.0, 0.0)
    rows = jnp.concatenate([first, head, jnp.zeros((4, width), F32)], axis=0)
    out_ref[...] = lax.dot_general(
        rows, factors, (((0,), (0,)), ((), ())), preferred_element_type=F32, precision=lax.Precision.HIGHEST
    )


def final_kernel(own_mid, other_mid, own_in, other_in, out_ref, in_hbm, mid_hbm, out_hbm, sems, *, n_tile):
    kept = kept_half(lax.axis_index("tile"), n_tile)
    half_mid = mid_hbm.shape[0] // 2
    half_in = in_hbm.shape[0] // 2
    moves = []
    for source, place, size, half in (
        (own_mid, mid_hbm, half_mid, kept),
        (other_mid, mid_hbm, half_mid, 1 - kept),
        (own_in, in_hbm, half_in, kept),
        (other_in, in_hbm, half_in, 1 - kept),
    ):
        moves.append(
            pltpu.make_async_copy(
                source.at[pl.ds(0, size)],
                place.at[pl.ds(pl.multiple_of(half * size, size), size)],
                sems.at[len(moves)],
            )
        )
    moves.append(pltpu.make_async_copy(out_ref, out_hbm, sems.at[len(moves)]))
    for move in moves:
        move.start()
    for move in moves:
        move.wait()


def kept_half(tile, n_tile):
    half = tile & 1
    shift = 1
    while (1 << shift) < n_tile:
        half = half ^ ((tile >> shift) & 1)
        shift += 1
    return half


def joined(own, got, own_first):
    first = jnp.where(own_first, own, got)
    second = jnp.where(own_first, got, own)
    row = lax.broadcasted_iota(jnp.int32, own.shape, 1)
    return first[:, 0:1] * second + jnp.where(row == 0, 0.0, first)


def pairs(size, bit):
    return [(i, i ^ bit) for i in range(size)]


def make_body(n_slab, n_tile):

    def body(
        encoded, spacing, counts, seg_first, seg_last, direction,
        field_in, field_mid, field_out, color_head, target,
    ):
        _, samples, rays, width = encoded.shape
        hidden = field_mid.shape[1]
        features = field_out.shape[2]
        count = samples * rays
        n_bits = (n_slab - 1).bit_length()
        row = lambda a: a.reshape(1, rays)
        seg_rows = 8 * ((4 + n_bits + 7) // 8)
        seg, *kept = pl.pallas_call(
            functools.partial(forward_kernel, n_bits=n_bits),
            name="forward",
            out_shape=(
                pltpu.VMEM((seg_rows, rays), F32),
                pltpu.VMEM((count, width), BF16),
                pltpu.VMEM((count, hidden), BF16),
                pltpu.VMEM((count, hidden), BF16),
                pltpu.VMEM((6, samples, rays), F32),
                pltpu.VMEM((16, hidden), BF16),
                pltpu.VMEM((hidden, hidden), BF16),
                pltpu.VMEM((3, rays), F32),
            ),
            in_specs=[HBM] * 11,
            out_specs=(VMEM,) * 8,
            scratch_shapes=[
                pltpu.VMEM((width, hidden), BF16),
                pltpu.VMEM((features, hidden), BF16),
                pltpu.VMEM((3, features), F32),
                pltpu.VMEM((samples, rays), F32),
                pltpu.VMEM((1, rays), jnp.int32),
                pltpu.VMEM((1, rays), jnp.int32),
                pltpu.VMEM((1, rays), jnp.int32),
                pltpu.VMEM((1, rays), jnp.int32),
                pltpu.VMEM((samples, 8, rays), F32),
                pltpu.SemaphoreType.DMA((12,)),
            ],
            compiler_params=LIMIT,
        )(
            *(
                pltpu.with_memory_space_constraint(a, pltpu.HBM)
                for a in (
                    encoded[0].reshape(count, width), spacing[0], counts, row(seg_first), row(seg_last),
                    row(direction), target.T, field_in[0], field_mid[0], field_out[0].T, color_head.T,
                )
            ),
        )

        both = jnp.stack([seg, lax.ppermute(seg, "tile", pairs(n_tile, 1))])
        block = both[:, :4]
        pieces = []
        for bit in range(n_bits):
            got = lax.ppermute(block, ("slab", "tile"), pairs(n_slab * n_tile, (n_tile << bit) | 1))
            pieces.append(got)
            if bit + 1 < n_bits:
                block = joined(block, got[::-1], both[:, 4 + bit : 5 + bit] > 0)

        x, h1, h2, save, w16, w2, target_rows = kept
        half_mid, half_in = hidden // 2, width // 2 + 8
        front, keep_mid, send_mid, back_one, factors = pl.pallas_call(
            functools.partial(backward_kernel, n_bits=n_bits, n_tile=n_tile),
            name="backward",
            out_shape=(
                pltpu.HBM((1, rays), F32),
                pltpu.VMEM((half_mid, hidden), F32),
                pltpu.VMEM((half_mid, hidden), F32),
                pltpu.VMEM((count, hidden), BF16),
                pltpu.VMEM((16, count), BF16),
            ),
            in_specs=[VMEM] * (7 + n_bits),
            out_specs=(HBM, VMEM, VMEM, VMEM, VMEM),
            scratch_shapes=[
                pltpu.VMEM((1, rays), F32),
                pltpu.VMEM((samples, 8, rays), F32),
                pltpu.VMEM((hidden, hidden), F32),
                pltpu.SemaphoreType.DMA,
            ],
            compiler_params=LIMIT,
            cost_estimate=pl.CostEstimate(flops=4 * count * hidden * hidden, bytes_accessed=0, transcendentals=0),
        )(seg, h1, h2, save, w16, w2, target_rows, *pieces)
        def chip_sum(keep, send):
            return keep + lax.ppermute(send, "tile", pairs(n_tile, 1))

        def tile_sum(part):
            bit = 2
            while bit < n_tile:
                part = part + lax.ppermute(part, "tile", pairs(n_tile, bit | 1))
                bit *= 2
            return part, lax.ppermute(part, "tile", pairs(n_tile, 1))

        part_mid = chip_sum(keep_mid, send_mid)
        keep_in, send_in = pl.pallas_call(
            functools.partial(first_kernel, n_tile=n_tile),
            name="first",
            out_shape=(pltpu.VMEM((half_in, hidden), F32), pltpu.VMEM((half_in, hidden), F32)),
            in_specs=[VMEM] * 4,
            out_specs=(VMEM, VMEM),
            scratch_shapes=[pltpu.VMEM((width, hidden), F32), pltpu.VMEM((16, hidden), F32)],
            compiler_params=LIMIT,
            cost_estimate=pl.CostEstimate(flops=4 * count * hidden * hidden, bytes_accessed=0, transcendentals=0),
        )(x, back_one, h2, factors)

        part_mid, keep_in, send_in = lax.optimization_barrier((part_mid, keep_in, send_in))
        own_mid, other_mid = tile_sum(part_mid)
        own_in, other_in = tile_sum(chip_sum(keep_in, send_in))
        expanded = pl.pallas_call(
            expand_kernel,
            name="expand",
            out_shape=pltpu.VMEM((features, hidden), F32),
            in_specs=[VMEM] * 2,
            out_specs=VMEM,
            compiler_params=LIMIT,
            cost_estimate=pl.CostEstimate(flops=2 * 8 * features * hidden * 6, bytes_accessed=0, transcendentals=0),
        )(own_in, color_head.T)
        grad_in, grad_mid, grad_out = pl.pallas_call(
            functools.partial(final_kernel, n_tile=n_tile),
            name="final",
            out_shape=(
                pltpu.HBM((width, hidden), F32),
                pltpu.HBM((hidden, hidden), F32),
                pltpu.HBM((features, hidden), F32),
            ),
            in_specs=[VMEM] * 5,
            out_specs=(HBM,) * 3,
            scratch_shapes=[pltpu.SemaphoreType.DMA((5,))],
            compiler_params=LIMIT,
        )(own_mid, other_mid, own_in, other_in, expanded)
        return front, grad_in[None], grad_mid[None], grad_out.T[None]

    return body


def solution(mesh):
    return jax.shard_map(
        make_body(mesh.shape["slab"], mesh.shape["tile"]),
        mesh=mesh,
        in_specs=(
            P("slab", None, "tile", None),
            P("slab", None, "tile"),
            P("slab", "tile"),
            P("tile"),
            P("tile"),
            P("tile"),
            P("slab", None, None),
            P("slab", None, None),
            P("slab", None, None),
            P(),
            P("tile", None),
        ),
        out_specs=(
            P("slab", "tile"),
            P("slab", None, None),
            P("slab", None, None),
            P("slab", None, None),
        ),
        check_vma=False,
    )
```

```python
import functools

import jax
import jax.numpy as jnp
from jax import lax
from jax.experimental import pallas as pl
from jax.experimental.pallas import tpu as pltpu
from jax.sharding import PartitionSpec as P

F32 = jnp.float32
BF16 = jnp.bfloat16
VMEM = pl.BlockSpec(memory_space=pltpu.VMEM)
HBM = pl.BlockSpec(memory_space=pltpu.HBM)
LIMIT = pltpu.CompilerParams(vmem_limit_bytes=32 * 1024 * 1024)
FIRST_LOAD = 4
BACKWARD_CHUNKS = 8
FIRST_CHUNKS = 8


def dot_nn(a, b):
    return lax.dot_general(a, b, (((1,), (0,)), ((), ())), preferred_element_type=F32)


def dot_nt(a, b):
    return lax.dot_general(a, b, (((1,), (1,)), ((), ())), preferred_element_type=F32)


def dot_tn(a, b):
    return lax.dot_general(a, b, (((0,), (0,)), ((), ())), preferred_element_type=F32)


def running_sum(values):
    rows = values.shape[0]
    ids = lax.broadcasted_iota(jnp.int32, values.shape, 0)
    shift = 1
    while shift < rows:
        moved = pltpu.roll(values, shift, 0)
        values = values + jnp.where(ids >= shift, moved, 0.0)
        shift *= 2
    return values


def split_three(values):
    high = values.astype(BF16)
    rest = values - high.astype(F32)
    mid = rest.astype(BF16)
    low = (rest - mid.astype(F32)).astype(BF16)
    return high, mid, low


def projection(head, field_out):
    first = jnp.where(lax.broadcasted_iota(jnp.int32, (1, head.shape[1]), 1) == 0, 1.0, 0.0).astype(BF16)
    density = dot_nn(first, field_out)
    high, mid, low = split_three(head)
    proj = dot_nn(high, field_out) + (dot_nn(mid, field_out) + dot_nn(low, field_out))
    proj_high = proj.astype(BF16).astype(F32)
    rest = proj - proj_high
    eight = jnp.concatenate([density, proj_high, rest, jnp.zeros_like(density)], axis=0)
    return jnp.concatenate([eight, eight], axis=0).astype(BF16)


def positive(values):
    rounded = values.astype(BF16)
    return jnp.maximum(rounded, jnp.zeros_like(rounded))


def where_positive(mask, values):
    rounded = values.astype(BF16)
    return jnp.where(mask > 0, rounded, jnp.zeros_like(rounded))


def forward_kernel(
    x_hbm, spacing_hbm, counts_hbm, first_hbm, last_hbm, direction_hbm, target_hbm,
    w1_hbm, w2_hbm, w3_hbm, head_hbm,
    seg_ref, x_ref, h1_ref, h2_ref, save_ref, w16_ref, w2_ref, target_ref,
    w1_ref, w3_ref, head_ref, spacing_ref, counts_ref, first_ref, last_ref, direction_ref, out8, sems, *, n_bits,
):
    samples, _, rays = out8.shape
    count = x_ref.shape[0]
    first_rows = min(FIRST_LOAD, samples) * rays
    moves = [
        pltpu.make_async_copy(source, place, sems.at[i])
        for i, (source, place) in enumerate(
            (
                (head_hbm, head_ref), (w3_hbm, w3_ref), (w1_hbm, w1_ref), (w2_hbm, w2_ref),
                (spacing_hbm, spacing_ref), (counts_hbm, counts_ref), (first_hbm, first_ref),
                (last_hbm, last_ref), (direction_hbm, direction_ref), (target_hbm, target_ref),
            )
        )
    ]
    loads = [
        pltpu.make_async_copy(x_hbm.at[pl.ds(at, size)], x_ref.at[pl.ds(at, size)], sems.at[len(moves) + i])
        for i, (at, size) in enumerate(((0, first_rows), (first_rows, count - first_rows)))
    ]
    for move in moves[2:3] + loads[:1] + moves[3:4] + moves[:2] + loads[1:] + moves[4:]:
        move.start()
    for move in moves[:4] + loads[:1]:
        move.wait()
    w16_ref[...] = projection(head_ref[...], w3_ref[...])

    for c in range(samples + 2):
        if c == first_rows // rays:
            for move in moves[4:] + loads[1:]:
                move.wait()
        if c < samples:
            rows = pl.ds(c * rays, rays)
            h1_ref[rows] = positive(dot_nn(x_ref[rows], w1_ref[...]))
        if 0 <= c - 1 < samples:
            rows = pl.ds((c - 1) * rays, rays)
            h2_ref[rows] = positive(dot_nn(h1_ref[rows], w2_ref[...]))
        if 0 <= c - 2 < samples:
            out8[c - 2] = dot_nt(w16_ref[...], h2_ref[pl.ds((c - 2) * rays, rays)])[:8]

    slab = lax.axis_index("slab")
    reverse = jnp.minimum(jnp.maximum(direction_ref[...], 0), 1)
    ahead = [(1 - (reverse ^ ((slab >> bit) & 1))).astype(F32) for bit in range(n_bits)]
    ahead += [jnp.zeros_like(ahead[0])] * (seg_ref.shape[0] - 4 - n_bits)
    density = out8[:, 0, :]
    proj = [out8[:, 1 + k, :] + out8[:, 4 + k, :] for k in range(3)]
    ids = lax.broadcasted_iota(jnp.int32, density.shape, 0)
    active = (first_ref[...] <= slab) & (slab < last_ref[...])
    live = jnp.where((ids < counts_ref[...]) & active, 1.0, 0.0)
    span = spacing_ref[...] * live
    optical = (jnp.maximum(density, 0.0) + jnp.log1p(jnp.exp(-jnp.abs(density)))) * span
    running = running_sum(optical)
    column = running[samples - 1 : samples]
    before = jnp.where(direction_ref[...] > 0, column - running, running - optical)
    reach = jnp.exp(-before)
    passed = jnp.exp(-optical)
    weights = reach * (1.0 - passed)
    seg_ref[...] = jnp.concatenate(
        [jnp.exp(-column)] + [jnp.sum(weights * p, axis=0, keepdims=True) for p in proj] + ahead, axis=0
    )
    save_ref[0] = weights
    save_ref[1] = reach * passed
    save_ref[2] = span * jax.nn.sigmoid(density)
    for k in range(3):
        save_ref[3 + k] = proj[k]


def backward_kernel(
    own_ref, h1_ref, h2_ref, save_ref, w16_ref, w2_ref, target_ref, *refs, n_bits, n_tile,
):
    pieces = refs[:n_bits]
    front_hbm, keep_ref, send_ref, one_ref, q16, front_ref, q8, mid_ref, sem = refs[n_bits:]
    samples, _, rays = q8.shape
    count = h1_ref.shape[0]
    slab = lax.axis_index("slab")
    kept = kept_half(lax.axis_index("tile"), n_tile)

    front_trans = back_trans = jnp.ones((1, rays), F32)
    front_color = back_color = jnp.zeros((3, rays), F32)
    for bit in range(n_bits):
        behind = own_ref[4 + bit : 5 + bit] > 0
        piece = pieces[bit] if len(pieces[bit].shape) == 2 else pieces[bit].at[1]
        trans, color = piece[0:1], piece[1:4]
        front_color = jnp.where(behind, front_color, color + trans * front_color)
        front_trans = jnp.where(behind, front_trans, trans * front_trans)
        back_color = jnp.where(behind, back_color + back_trans * color, back_color)
        back_trans = jnp.where(behind, back_trans * trans, back_trans)
    forward_ray = own_ref[4:5] + (slab & 1).astype(F32) == 1.0
    front_ref[...] = front_trans
    store = pltpu.make_async_copy(front_ref, front_hbm, sem)
    store.start()
    own = own_ref[...]
    own_trans = own[0:1]
    logits = front_color + front_trans * own[1:4] + (front_trans * own_trans) * back_color
    shade = jax.nn.sigmoid(logits)
    error = (shade - target_ref[...]) / rays
    grad_logit = error * shade * (1.0 - shade)
    grad_trans = front_trans * jnp.sum(grad_logit * back_color, axis=0, keepdims=True)
    pull = front_trans * grad_logit

    weights = save_ref[0]
    grad_weight = pull[0:1] * save_ref[3] + pull[1:2] * save_ref[4] + pull[2:3] * save_ref[5]
    product = weights * grad_weight
    running = running_sum(product)
    total = running[samples - 1 : samples]
    after = jnp.where(forward_ray, total - running, running - product)
    grad_optical = grad_weight * save_ref[1] - after - grad_trans * own_trans
    q8[:, 0, :] = grad_optical * save_ref[2]
    for k in range(3):
        q = weights * pull[k : k + 1]
        q8[:, 1 + k, :] = q
        q8[:, 4 + k, :] = q
    q8[:, 7, :] = jnp.zeros_like(weights)
    for j in range(samples):
        rows = q8[j]
        high = rows.astype(BF16).astype(F32)
        q16[:, j * rays : (j + 1) * rays] = jnp.concatenate([high, rows - high], axis=0).astype(BF16)

    chunk = count // BACKWARD_CHUNKS
    def back_two(c):
        rows = pl.ds(c * chunk, chunk)
        return where_positive(h2_ref[rows], dot_tn(q16[:, rows], w16_ref[...]))

    later = back_two(0)
    for c in range(BACKWARD_CHUNKS):
        rows = pl.ds(c * chunk, chunk)
        now = later
        if c + 1 < BACKWARD_CHUNKS:
            later = back_two(c + 1)
        grad_mid = dot_tn(h1_ref[rows], now)
        mid_ref[...] = grad_mid if c == 0 else mid_ref[...] + grad_mid
        one_ref[rows] = where_positive(h1_ref[rows], dot_nt(now, w2_ref[...]))

    half = mid_ref.shape[0] // 2
    for place, which in ((send_ref, 1 - kept), (keep_ref, kept)):
        place[...] = mid_ref[pl.ds(pl.multiple_of(which * half, half), half)]
    store.wait()


def first_kernel(x_ref, one_ref, h2_ref, q16, keep_ref, send_ref, in_ref, out_ref, *, n_tile):
    kept = kept_half(lax.axis_index("tile"), n_tile)
    count = x_ref.shape[0]
    chunk = count // FIRST_CHUNKS
    for c in range(FIRST_CHUNKS):
        rows = pl.ds(c * chunk, chunk)
        grad_in = dot_tn(x_ref[rows], one_ref[rows])
        grad_out = dot_nn(q16[:, rows], h2_ref[rows])
        for ref, part in ((out_ref, grad_out), (in_ref, grad_in)):
            ref[...] = part if c == 0 else ref[...] + part

    half = in_ref.shape[0] // 2
    for place, which in ((send_ref, 1 - kept), (keep_ref, kept)):
        place[:half] = in_ref[pl.ds(pl.multiple_of(which * half, half), half)]
        place[half:] = out_ref[:8] + out_ref[8:]


def expand_kernel(factors_ref, head_ref, out_ref):
    factors = factors_ref[factors_ref.shape[0] - 8 :]
    head = head_ref[...]
    width = head.shape[1]
    first = jnp.where(lax.broadcasted_iota(jnp.int32, (1, width), 1) == 0, 1.0, 0.0)
    rows = jnp.concatenate([first, head, jnp.zeros((4, width), F32)], axis=0)
    out_ref[...] = lax.dot_general(
        rows, factors, (((0,), (0,)), ((), ())), preferred_element_type=F32, precision=lax.Precision.HIGHEST
    )


def final_kernel(own_mid, other_mid, own_in, other_in, out_ref, in_hbm, mid_hbm, out_hbm, sems, *, n_tile):
    kept = kept_half(lax.axis_index("tile"), n_tile)
    half_mid = mid_hbm.shape[0] // 2
    half_in = in_hbm.shape[0] // 2
    moves = []
    for source, place, size, half in (
        (own_mid, mid_hbm, half_mid, kept),
        (other_mid, mid_hbm, half_mid, 1 - kept),
        (own_in, in_hbm, half_in, kept),
        (other_in, in_hbm, half_in, 1 - kept),
    ):
        moves.append(
            pltpu.make_async_copy(
                source.at[pl.ds(0, size)],
                place.at[pl.ds(pl.multiple_of(half * size, size), size)],
                sems.at[len(moves)],
            )
        )
    moves.append(pltpu.make_async_copy(out_ref, out_hbm, sems.at[len(moves)]))
    for move in moves:
        move.start()
    for move in moves:
        move.wait()


def kept_half(tile, n_tile):
    half = tile & 1
    shift = 1
    while (1 << shift) < n_tile:
        half = half ^ ((tile >> shift) & 1)
        shift += 1
    return half


def join_kernel(seg_ref, other_ref, block_ref, got_ref, out_ref, *, bit):
    wanted = (0, 1) if len(out_ref.shape) == 3 else (1,)
    for i in wanted:
        own, got = block_ref[i], got_ref[1 - i]
        own_trans, got_trans = own[0:1], got[0:1]
        ahead = (other_ref if i else seg_ref)[4 + bit : 5 + bit] > 0
        color = jnp.where(ahead, own + own_trans * got, got + got_trans * own)
        row = lax.broadcasted_iota(jnp.int32, own.shape, 0)
        result = jnp.where(row == 0, own_trans * got_trans, color)
        if len(wanted) == 2:
            out_ref[i] = result
        else:
            out_ref[...] = result


def pairs(size, bit):
    return [(i, i ^ bit) for i in range(size)]


def make_body(n_slab, n_tile):

    def body(
        encoded, spacing, counts, seg_first, seg_last, direction,
        field_in, field_mid, field_out, color_head, target,
    ):
        _, samples, rays, width = encoded.shape
        hidden = field_mid.shape[1]
        features = field_out.shape[2]
        count = samples * rays
        n_bits = (n_slab - 1).bit_length()
        row = lambda a: a.reshape(1, rays)
        seg_rows = 8 * ((4 + n_bits + 7) // 8)
        seg, *kept = pl.pallas_call(
            functools.partial(forward_kernel, n_bits=n_bits),
            name="forward",
            out_shape=(
                pltpu.VMEM((seg_rows, rays), F32),
                pltpu.VMEM((count, width), BF16),
                pltpu.VMEM((count, hidden), BF16),
                pltpu.VMEM((count, hidden), BF16),
                pltpu.VMEM((6, samples, rays), F32),
                pltpu.VMEM((16, hidden), BF16),
                pltpu.VMEM((hidden, hidden), BF16),
                pltpu.VMEM((3, rays), F32),
            ),
            in_specs=[HBM] * 11,
            out_specs=(VMEM,) * 8,
            scratch_shapes=[
                pltpu.VMEM((width, hidden), BF16),
                pltpu.VMEM((features, hidden), BF16),
                pltpu.VMEM((3, features), F32),
                pltpu.VMEM((samples, rays), F32),
                pltpu.VMEM((1, rays), jnp.int32),
                pltpu.VMEM((1, rays), jnp.int32),
                pltpu.VMEM((1, rays), jnp.int32),
                pltpu.VMEM((1, rays), jnp.int32),
                pltpu.VMEM((samples, 8, rays), F32),
                pltpu.SemaphoreType.DMA((12,)),
            ],
            compiler_params=LIMIT,
        )(
            *(
                pltpu.with_memory_space_constraint(a, pltpu.HBM)
                for a in (
                    encoded[0].reshape(count, width), spacing[0], counts, row(seg_first), row(seg_last),
                    row(direction), target.T, field_in[0], field_mid[0], field_out[0].T, color_head.T,
                )
            ),
        )

        other = lax.ppermute(seg, "tile", pairs(n_tile, 1))
        block = jnp.stack([seg[:4], other[:4]])
        pieces = []
        for bit in range(n_bits):
            got = lax.ppermute(block, ("slab", "tile"), pairs(n_slab * n_tile, (n_tile << bit) | 1))
            pieces.append(got)
            if bit + 1 < n_bits:
                shape = (2, 4, rays) if bit + 2 < n_bits else (4, rays)
                block = pl.pallas_call(
                    functools.partial(join_kernel, bit=bit),
                    name="join",
                    out_shape=pltpu.VMEM(shape, F32),
                    in_specs=[VMEM] * 4,
                    out_specs=VMEM,
                    compiler_params=LIMIT,
                )(seg, other, block, got)

        x, h1, h2, save, w16, w2, target_rows = kept
        half_mid, half_in = hidden // 2, width // 2 + 8
        front, keep_mid, send_mid, back_one, factors = pl.pallas_call(
            functools.partial(backward_kernel, n_bits=n_bits, n_tile=n_tile),
            name="backward",
            out_shape=(
                pltpu.HBM((1, rays), F32),
                pltpu.VMEM((half_mid, hidden), F32),
                pltpu.VMEM((half_mid, hidden), F32),
                pltpu.VMEM((count, hidden), BF16),
                pltpu.VMEM((16, count), BF16),
            ),
            in_specs=[VMEM] * (7 + n_bits),
            out_specs=(HBM, VMEM, VMEM, VMEM, VMEM),
            scratch_shapes=[
                pltpu.VMEM((1, rays), F32),
                pltpu.VMEM((samples, 8, rays), F32),
                pltpu.VMEM((hidden, hidden), F32),
                pltpu.SemaphoreType.DMA,
            ],
            compiler_params=LIMIT,
            cost_estimate=pl.CostEstimate(flops=4 * count * hidden * hidden, bytes_accessed=0, transcendentals=0),
        )(seg, h1, h2, save, w16, w2, target_rows, *pieces)
        def chip_sum(keep, send):
            return keep + lax.ppermute(send, "tile", pairs(n_tile, 1))

        def tile_sum(part):
            bit = 2
            while bit < n_tile:
                part = part + lax.ppermute(part, "tile", pairs(n_tile, bit | 1))
                bit *= 2
            return part, lax.ppermute(part, "tile", pairs(n_tile, 1))

        part_mid = chip_sum(keep_mid, send_mid)
        keep_in, send_in = pl.pallas_call(
            functools.partial(first_kernel, n_tile=n_tile),
            name="first",
            out_shape=(pltpu.VMEM((half_in, hidden), F32), pltpu.VMEM((half_in, hidden), F32)),
            in_specs=[VMEM] * 4,
            out_specs=(VMEM, VMEM),
            scratch_shapes=[pltpu.VMEM((width, hidden), F32), pltpu.VMEM((16, hidden), F32)],
            compiler_params=LIMIT,
            cost_estimate=pl.CostEstimate(flops=4 * count * hidden * hidden, bytes_accessed=0, transcendentals=0),
        )(x, back_one, h2, factors)

        part_mid, keep_in, send_in = lax.optimization_barrier((part_mid, keep_in, send_in))
        own_mid, other_mid = tile_sum(part_mid)
        own_in, other_in = tile_sum(chip_sum(keep_in, send_in))
        expanded = pl.pallas_call(
            expand_kernel,
            name="expand",
            out_shape=pltpu.VMEM((features, hidden), F32),
            in_specs=[VMEM] * 2,
            out_specs=VMEM,
            compiler_params=LIMIT,
            cost_estimate=pl.CostEstimate(flops=2 * 8 * features * hidden * 6, bytes_accessed=0, transcendentals=0),
        )(own_in, color_head.T)
        grad_in, grad_mid, grad_out = pl.pallas_call(
            functools.partial(final_kernel, n_tile=n_tile),
            name="final",
            out_shape=(
                pltpu.HBM((width, hidden), F32),
                pltpu.HBM((hidden, hidden), F32),
                pltpu.HBM((features, hidden), F32),
            ),
            in_specs=[VMEM] * 5,
            out_specs=(HBM,) * 3,
            scratch_shapes=[pltpu.SemaphoreType.DMA((5,))],
            compiler_params=LIMIT,
        )(own_mid, other_mid, own_in, other_in, expanded)
        return front, grad_in[None], grad_mid[None], grad_out.T[None]

    return body


def solution(mesh):
    return jax.shard_map(
        make_body(mesh.shape["slab"], mesh.shape["tile"]),
        mesh=mesh,
        in_specs=(
            P("slab", None, "tile", None),
            P("slab", None, "tile"),
            P("slab", "tile"),
            P("tile"),
            P("tile"),
            P("tile"),
            P("slab", None, None),
            P("slab", None, None),
            P("slab", None, None),
            P(),
            P("tile", None),
        ),
        out_specs=(
            P("slab", "tile"),
            P("slab", None, None),
            P("slab", None, None),
            P("slab", None, None),
        ),
        check_vma=False,
    )
```

```python
import functools

import jax
import jax.numpy as jnp
from jax import lax
from jax.experimental import pallas as pl
from jax.experimental.pallas import tpu as pltpu
from jax.sharding import PartitionSpec as P

F32 = jnp.float32
BF16 = jnp.bfloat16
VMEM = pl.BlockSpec(memory_space=pltpu.VMEM)
HBM = pl.BlockSpec(memory_space=pltpu.HBM)
LIMIT = pltpu.CompilerParams(vmem_limit_bytes=32 * 1024 * 1024)
FIRST_LOAD = 4
BACKWARD_CHUNKS = 8
FIRST_CHUNKS = 8


def dot_nn(a, b):
    return lax.dot_general(a, b, (((1,), (0,)), ((), ())), preferred_element_type=F32)


def dot_nt(a, b):
    return lax.dot_general(a, b, (((1,), (1,)), ((), ())), preferred_element_type=F32)


def dot_tn(a, b):
    return lax.dot_general(a, b, (((0,), (0,)), ((), ())), preferred_element_type=F32)


def running_sum(values):
    rows = values.shape[0]
    ids = lax.broadcasted_iota(jnp.int32, values.shape, 0)
    shift = 1
    while shift < rows:
        moved = pltpu.roll(values, shift, 0)
        values = values + jnp.where(ids >= shift, moved, 0.0)
        shift *= 2
    return values


def split_three(values):
    high = values.astype(BF16)
    rest = values - high.astype(F32)
    mid = rest.astype(BF16)
    low = (rest - mid.astype(F32)).astype(BF16)
    return high, mid, low


def projection(head, field_out):
    first = jnp.where(lax.broadcasted_iota(jnp.int32, (1, head.shape[1]), 1) == 0, 1.0, 0.0).astype(BF16)
    density = dot_nn(first, field_out)
    high, mid, low = split_three(head)
    proj = dot_nn(high, field_out) + (dot_nn(mid, field_out) + dot_nn(low, field_out))
    proj_high = proj.astype(BF16).astype(F32)
    rest = proj - proj_high
    eight = jnp.concatenate([density, proj_high, rest, jnp.zeros_like(density)], axis=0)
    return jnp.concatenate([eight, eight], axis=0).astype(BF16)


def positive(values):
    rounded = values.astype(BF16)
    return jnp.maximum(rounded, jnp.zeros_like(rounded))


def where_positive(mask, values):
    rounded = values.astype(BF16)
    return jnp.where(mask > 0, rounded, jnp.zeros_like(rounded))


def forward_kernel(
    x_hbm, spacing_hbm, counts_hbm, first_hbm, last_hbm, direction_hbm, target_hbm,
    w1_hbm, w2_hbm, w3_hbm, head_hbm,
    seg_ref, x_ref, h1_ref, h2_ref, save_ref, w16_ref, w2_ref, target_ref,
    w1_ref, w3_ref, head_ref, spacing_ref, counts_ref, first_ref, last_ref, direction_ref, out8, sems, *, n_bits,
):
    samples, _, rays = out8.shape
    count = x_ref.shape[0]
    first_rows = min(FIRST_LOAD, samples) * rays
    moves = [
        pltpu.make_async_copy(source, place, sems.at[i])
        for i, (source, place) in enumerate(
            (
                (head_hbm, head_ref), (w3_hbm, w3_ref), (w1_hbm, w1_ref), (w2_hbm, w2_ref),
                (spacing_hbm, spacing_ref), (counts_hbm, counts_ref), (first_hbm, first_ref),
                (last_hbm, last_ref), (direction_hbm, direction_ref), (target_hbm, target_ref),
            )
        )
    ]
    loads = [
        pltpu.make_async_copy(x_hbm.at[pl.ds(at, size)], x_ref.at[pl.ds(at, size)], sems.at[len(moves) + i])
        for i, (at, size) in enumerate(((0, first_rows), (first_rows, count - first_rows)))
    ]
    for move in moves[2:3] + loads[:1] + moves[3:4] + moves[:2] + loads[1:] + moves[4:]:
        move.start()
    for move in moves[:4] + loads[:1]:
        move.wait()

    for c in range(samples + 2):
        if c == first_rows // rays:
            for move in moves[4:] + loads[1:]:
                move.wait()
        if c < samples:
            rows = pl.ds(c * rays, rays)
            h1_ref[rows] = positive(dot_nn(x_ref[rows], w1_ref[...]))
        if 0 <= c - 1 < samples:
            rows = pl.ds((c - 1) * rays, rays)
            h2_ref[rows] = positive(dot_nn(h1_ref[rows], w2_ref[...]))
        if c == 2:
            w16_ref[...] = projection(head_ref[...], w3_ref[...])
        if 0 <= c - 2 < samples:
            out8[c - 2] = dot_nt(w16_ref[...], h2_ref[pl.ds((c - 2) * rays, rays)])[:8]

    slab = lax.axis_index("slab")
    reverse = jnp.minimum(jnp.maximum(direction_ref[...], 0), 1)
    ahead = [(1 - (reverse ^ ((slab >> bit) & 1))).astype(F32) for bit in range(n_bits)]
    ahead += [jnp.zeros_like(ahead[0])] * (seg_ref.shape[0] - 4 - n_bits)
    density = out8[:, 0, :]
    proj = [out8[:, 1 + k, :] + out8[:, 4 + k, :] for k in range(3)]
    ids = lax.broadcasted_iota(jnp.int32, density.shape, 0)
    active = (first_ref[...] <= slab) & (slab < last_ref[...])
    live = jnp.where((ids < counts_ref[...]) & active, 1.0, 0.0)
    span = spacing_ref[...] * live
    optical = (jnp.maximum(density, 0.0) + jnp.log1p(jnp.exp(-jnp.abs(density)))) * span
    running = running_sum(optical)
    column = running[samples - 1 : samples]
    before = jnp.where(direction_ref[...] > 0, column - running, running - optical)
    reach = jnp.exp(-before)
    passed = jnp.exp(-optical)
    weights = reach * (1.0 - passed)
    seg_ref[...] = jnp.concatenate(
        [jnp.exp(-column)] + [jnp.sum(weights * p, axis=0, keepdims=True) for p in proj] + ahead, axis=0
    )
    save_ref[0] = weights
    save_ref[1] = reach * passed
    save_ref[2] = span * jax.nn.sigmoid(density)
    for k in range(3):
        save_ref[3 + k] = proj[k]


def backward_kernel(
    own_ref, h1_ref, h2_ref, save_ref, w16_ref, w2_ref, target_ref, *refs, n_bits, n_tile,
):
    pieces = refs[:n_bits]
    front_hbm, keep_ref, send_ref, one_ref, q16, front_ref, q8, mid_ref, sem = refs[n_bits:]
    samples, _, rays = q8.shape
    count = h1_ref.shape[0]
    slab = lax.axis_index("slab")
    kept = kept_half(lax.axis_index("tile"), n_tile)

    front_trans = back_trans = jnp.ones((1, rays), F32)
    front_color = back_color = jnp.zeros((3, rays), F32)
    for bit in range(n_bits):
        behind = own_ref[4 + bit : 5 + bit] > 0
        piece = pieces[bit] if len(pieces[bit].shape) == 2 else pieces[bit].at[1]
        trans, color = piece[0:1], piece[1:4]
        front_color = jnp.where(behind, front_color, color + trans * front_color)
        front_trans = jnp.where(behind, front_trans, trans * front_trans)
        back_color = jnp.where(behind, back_color + back_trans * color, back_color)
        back_trans = jnp.where(behind, back_trans * trans, back_trans)
    forward_ray = own_ref[4:5] + (slab & 1).astype(F32) == 1.0
    front_ref[...] = front_trans
    store = pltpu.make_async_copy(front_ref, front_hbm, sem)
    store.start()
    own = own_ref[...]
    own_trans = own[0:1]
    logits = front_color + front_trans * own[1:4] + (front_trans * own_trans) * back_color
    shade = jax.nn.sigmoid(logits)
    error = (shade - target_ref[...]) / rays
    grad_logit = error * shade * (1.0 - shade)
    grad_trans = front_trans * jnp.sum(grad_logit * back_color, axis=0, keepdims=True)
    pull = front_trans * grad_logit

    weights = save_ref[0]
    grad_weight = pull[0:1] * save_ref[3] + pull[1:2] * save_ref[4] + pull[2:3] * save_ref[5]
    product = weights * grad_weight
    running = running_sum(product)
    total = running[samples - 1 : samples]
    after = jnp.where(forward_ray, total - running, running - product)
    grad_optical = grad_weight * save_ref[1] - after - grad_trans * own_trans
    q8[:, 0, :] = grad_optical * save_ref[2]
    for k in range(3):
        q = weights * pull[k : k + 1]
        q8[:, 1 + k, :] = q
        q8[:, 4 + k, :] = q
    q8[:, 7, :] = jnp.zeros_like(weights)
    for j in range(samples):
        rows = q8[j]
        high = rows.astype(BF16).astype(F32)
        q16[:, j * rays : (j + 1) * rays] = jnp.concatenate([high, rows - high], axis=0).astype(BF16)

    chunk = count // BACKWARD_CHUNKS
    def back_two(c):
        rows = pl.ds(c * chunk, chunk)
        return where_positive(h2_ref[rows], dot_tn(q16[:, rows], w16_ref[...]))

    later = back_two(0)
    for c in range(BACKWARD_CHUNKS):
        rows = pl.ds(c * chunk, chunk)
        now = later
        if c + 1 < BACKWARD_CHUNKS:
            later = back_two(c + 1)
        grad_mid = dot_tn(h1_ref[rows], now)
        mid_ref[...] = grad_mid if c == 0 else mid_ref[...] + grad_mid
        one_ref[rows] = where_positive(h1_ref[rows], dot_nt(now, w2_ref[...]))

    half = mid_ref.shape[0] // 2
    for place, which in ((send_ref, 1 - kept), (keep_ref, kept)):
        place[...] = mid_ref[pl.ds(pl.multiple_of(which * half, half), half)]
    store.wait()


def first_kernel(x_ref, one_ref, h2_ref, q16, keep_ref, send_ref, in_ref, out_ref, *, n_tile):
    kept = kept_half(lax.axis_index("tile"), n_tile)
    count = x_ref.shape[0]
    chunk = count // FIRST_CHUNKS
    for c in range(FIRST_CHUNKS):
        rows = pl.ds(c * chunk, chunk)
        grad_in = dot_tn(x_ref[rows], one_ref[rows])
        grad_out = dot_nn(q16[:, rows], h2_ref[rows])
        for ref, part in ((out_ref, grad_out), (in_ref, grad_in)):
            ref[...] = part if c == 0 else ref[...] + part

    half = in_ref.shape[0] // 2
    for place, which in ((send_ref, 1 - kept), (keep_ref, kept)):
        place[:half] = in_ref[pl.ds(pl.multiple_of(which * half, half), half)]
        place[half:] = out_ref[:8] + out_ref[8:]


def expand_kernel(factors_ref, head_ref, out_ref):
    factors = factors_ref[factors_ref.shape[0] - 8 :]
    head = head_ref[...]
    width = head.shape[1]
    first = jnp.where(lax.broadcasted_iota(jnp.int32, (1, width), 1) == 0, 1.0, 0.0)
    rows = jnp.concatenate([first, head, jnp.zeros((4, width), F32)], axis=0)
    out_ref[...] = lax.dot_general(
        rows, factors, (((0,), (0,)), ((), ())), preferred_element_type=F32, precision=lax.Precision.HIGHEST
    )


def final_kernel(own_mid, other_mid, own_in, other_in, out_ref, in_hbm, mid_hbm, out_hbm, sems, *, n_tile):
    kept = kept_half(lax.axis_index("tile"), n_tile)
    half_mid = mid_hbm.shape[0] // 2
    half_in = in_hbm.shape[0] // 2
    moves = []
    for source, place, size, half in (
        (own_mid, mid_hbm, half_mid, kept),
        (other_mid, mid_hbm, half_mid, 1 - kept),
        (own_in, in_hbm, half_in, kept),
        (other_in, in_hbm, half_in, 1 - kept),
    ):
        moves.append(
            pltpu.make_async_copy(
                source.at[pl.ds(0, size)],
                place.at[pl.ds(pl.multiple_of(half * size, size), size)],
                sems.at[len(moves)],
            )
        )
    moves.append(pltpu.make_async_copy(out_ref, out_hbm, sems.at[len(moves)]))
    for move in moves:
        move.start()
    for move in moves:
        move.wait()


def kept_half(tile, n_tile):
    half = tile & 1
    shift = 1
    while (1 << shift) < n_tile:
        half = half ^ ((tile >> shift) & 1)
        shift += 1
    return half


def join_kernel(seg_ref, other_ref, block_ref, got_ref, out_ref, *, bit):
    wanted = (0, 1) if len(out_ref.shape) == 3 else (1,)
    for i in wanted:
        own, got = block_ref[i], got_ref[1 - i]
        own_trans, got_trans = own[0:1], got[0:1]
        ahead = (other_ref if i else seg_ref)[4 + bit : 5 + bit] > 0
        color = jnp.where(ahead, own + own_trans * got, got + got_trans * own)
        row = lax.broadcasted_iota(jnp.int32, own.shape, 0)
        result = jnp.where(row == 0, own_trans * got_trans, color)
        if len(wanted) == 2:
            out_ref[i] = result
        else:
            out_ref[...] = result


def pairs(size, bit):
    return [(i, i ^ bit) for i in range(size)]


def make_body(n_slab, n_tile):

    def body(
        encoded, spacing, counts, seg_first, seg_last, direction,
        field_in, field_mid, field_out, color_head, target,
    ):
        _, samples, rays, width = encoded.shape
        hidden = field_mid.shape[1]
        features = field_out.shape[2]
        count = samples * rays
        n_bits = (n_slab - 1).bit_length()
        row = lambda a: a.reshape(1, rays)
        seg_rows = 8 * ((4 + n_bits + 7) // 8)
        seg, *kept = pl.pallas_call(
            functools.partial(forward_kernel, n_bits=n_bits),
            name="forward",
            out_shape=(
                pltpu.VMEM((seg_rows, rays), F32),
                pltpu.VMEM((count, width), BF16),
                pltpu.VMEM((count, hidden), BF16),
                pltpu.VMEM((count, hidden), BF16),
                pltpu.VMEM((6, samples, rays), F32),
                pltpu.VMEM((16, hidden), BF16),
                pltpu.VMEM((hidden, hidden), BF16),
                pltpu.VMEM((3, rays), F32),
            ),
            in_specs=[HBM] * 11,
            out_specs=(VMEM,) * 8,
            scratch_shapes=[
                pltpu.VMEM((width, hidden), BF16),
                pltpu.VMEM((features, hidden), BF16),
                pltpu.VMEM((3, features), F32),
                pltpu.VMEM((samples, rays), F32),
                pltpu.VMEM((1, rays), jnp.int32),
                pltpu.VMEM((1, rays), jnp.int32),
                pltpu.VMEM((1, rays), jnp.int32),
                pltpu.VMEM((1, rays), jnp.int32),
                pltpu.VMEM((samples, 8, rays), F32),
                pltpu.SemaphoreType.DMA((12,)),
            ],
            compiler_params=LIMIT,
        )(
            *(
                pltpu.with_memory_space_constraint(a, pltpu.HBM)
                for a in (
                    encoded[0].reshape(count, width), spacing[0], counts, row(seg_first), row(seg_last),
                    row(direction), target.T, field_in[0], field_mid[0], field_out[0].T, color_head.T,
                )
            ),
        )

        other = lax.ppermute(seg, "tile", pairs(n_tile, 1))
        block = jnp.stack([seg[:4], other[:4]])
        pieces = []
        for bit in range(n_bits):
            got = lax.ppermute(block, ("slab", "tile"), pairs(n_slab * n_tile, (n_tile << bit) | 1))
            pieces.append(got)
            if bit + 1 < n_bits:
                shape = (2, 4, rays)
                block = pl.pallas_call(
                    functools.partial(join_kernel, bit=bit),
                    name="join",
                    out_shape=pltpu.VMEM(shape, F32),
                    in_specs=[VMEM] * 4,
                    out_specs=VMEM,
                    compiler_params=LIMIT,
                )(seg, other, block, got)

        x, h1, h2, save, w16, w2, target_rows = kept
        half_mid, half_in = hidden // 2, width // 2 + 8
        front, keep_mid, send_mid, back_one, factors = pl.pallas_call(
            functools.partial(backward_kernel, n_bits=n_bits, n_tile=n_tile),
            name="backward",
            out_shape=(
                pltpu.HBM((1, rays), F32),
                pltpu.VMEM((half_mid, hidden), F32),
                pltpu.VMEM((half_mid, hidden), F32),
                pltpu.VMEM((count, hidden), BF16),
                pltpu.VMEM((16, count), BF16),
            ),
            in_specs=[VMEM] * (7 + n_bits),
            out_specs=(HBM, VMEM, VMEM, VMEM, VMEM),
            scratch_shapes=[
                pltpu.VMEM((1, rays), F32),
                pltpu.VMEM((samples, 8, rays), F32),
                pltpu.VMEM((hidden, hidden), F32),
                pltpu.SemaphoreType.DMA,
            ],
            compiler_params=LIMIT,
            cost_estimate=pl.CostEstimate(flops=4 * count * hidden * hidden, bytes_accessed=0, transcendentals=0),
        )(seg, h1, h2, save, w16, w2, target_rows, *pieces)
        def chip_sum(keep, send):
            return keep + lax.ppermute(send, "tile", pairs(n_tile, 1))

        def tile_sum(part):
            bit = 2
            while bit < n_tile:
                part = part + lax.ppermute(part, "tile", pairs(n_tile, bit | 1))
                bit *= 2
            return part, lax.ppermute(part, "tile", pairs(n_tile, 1))

        part_mid = chip_sum(keep_mid, send_mid)
        keep_in, send_in = pl.pallas_call(
            functools.partial(first_kernel, n_tile=n_tile),
            name="first",
            out_shape=(pltpu.VMEM((half_in, hidden), F32), pltpu.VMEM((half_in, hidden), F32)),
            in_specs=[VMEM] * 4,
            out_specs=(VMEM, VMEM),
            scratch_shapes=[pltpu.VMEM((width, hidden), F32), pltpu.VMEM((16, hidden), F32)],
            compiler_params=LIMIT,
            cost_estimate=pl.CostEstimate(flops=4 * count * hidden * hidden, bytes_accessed=0, transcendentals=0),
        )(x, back_one, h2, factors)

        part_mid, keep_in, send_in = lax.optimization_barrier((part_mid, keep_in, send_in))
        own_mid, other_mid = tile_sum(part_mid)
        own_in, other_in = tile_sum(chip_sum(keep_in, send_in))
        expanded = pl.pallas_call(
            expand_kernel,
            name="expand",
            out_shape=pltpu.VMEM((features, hidden), F32),
            in_specs=[VMEM] * 2,
            out_specs=VMEM,
            compiler_params=LIMIT,
            cost_estimate=pl.CostEstimate(flops=2 * 8 * features * hidden * 6, bytes_accessed=0, transcendentals=0),
        )(own_in, color_head.T)
        grad_in, grad_mid, grad_out = pl.pallas_call(
            functools.partial(final_kernel, n_tile=n_tile),
            name="final",
            out_shape=(
                pltpu.HBM((width, hidden), F32),
                pltpu.HBM((hidden, hidden), F32),
                pltpu.HBM((features, hidden), F32),
            ),
            in_specs=[VMEM] * 5,
            out_specs=(HBM,) * 3,
            scratch_shapes=[pltpu.SemaphoreType.DMA((5,))],
            compiler_params=LIMIT,
        )(own_mid, other_mid, own_in, other_in, expanded)
        return front, grad_in[None], grad_mid[None], grad_out.T[None]

    return body


def solution(mesh):
    return jax.shard_map(
        make_body(mesh.shape["slab"], mesh.shape["tile"]),
        mesh=mesh,
        in_specs=(
            P("slab", None, "tile", None),
            P("slab", None, "tile"),
            P("slab", "tile"),
            P("tile"),
            P("tile"),
            P("tile"),
            P("slab", None, None),
            P("slab", None, None),
            P("slab", None, None),
            P(),
            P("tile", None),
        ),
        out_specs=(
            P("slab", "tile"),
            P("slab", None, None),
            P("slab", None, None),
            P("slab", None, None),
        ),
        check_vma=False,
    )
```

```python
import functools

import jax
import jax.numpy as jnp
from jax import lax
from jax.experimental import pallas as pl
from jax.experimental.pallas import tpu as pltpu
from jax.sharding import PartitionSpec as P

F32 = jnp.float32
BF16 = jnp.bfloat16
VMEM = pl.BlockSpec(memory_space=pltpu.VMEM)
HBM = pl.BlockSpec(memory_space=pltpu.HBM)
LIMIT = pltpu.CompilerParams(vmem_limit_bytes=32 * 1024 * 1024)
FIRST_LOAD = 4
BACKWARD_CHUNKS = 8
FIRST_CHUNKS = 8


def dot_nn(a, b):
    return lax.dot_general(a, b, (((1,), (0,)), ((), ())), preferred_element_type=F32)


def dot_nt(a, b):
    return lax.dot_general(a, b, (((1,), (1,)), ((), ())), preferred_element_type=F32)


def dot_tn(a, b):
    return lax.dot_general(a, b, (((0,), (0,)), ((), ())), preferred_element_type=F32)


def running_sum(values):
    rows = values.shape[0]
    ids = lax.broadcasted_iota(jnp.int32, values.shape, 0)
    shift = 1
    while shift < rows:
        moved = pltpu.roll(values, shift, 0)
        values = values + jnp.where(ids >= shift, moved, 0.0)
        shift *= 2
    return values


def split_three(values):
    high = values.astype(BF16)
    rest = values - high.astype(F32)
    mid = rest.astype(BF16)
    low = (rest - mid.astype(F32)).astype(BF16)
    return high, mid, low


def projection(head, field_out):
    first = jnp.where(lax.broadcasted_iota(jnp.int32, (1, head.shape[1]), 1) == 0, 1.0, 0.0).astype(BF16)
    density = dot_nn(first, field_out)
    high, mid, low = split_three(head)
    proj = dot_nn(high, field_out) + (dot_nn(mid, field_out) + dot_nn(low, field_out))
    proj_high = proj.astype(BF16).astype(F32)
    rest = proj - proj_high
    eight = jnp.concatenate([density, proj_high, rest, jnp.zeros_like(density)], axis=0)
    return jnp.concatenate([eight, eight], axis=0).astype(BF16)


def positive(values):
    rounded = values.astype(BF16)
    return jnp.maximum(rounded, jnp.zeros_like(rounded))


def where_positive(mask, values):
    rounded = values.astype(BF16)
    return jnp.where(mask > 0, rounded, jnp.zeros_like(rounded))


def forward_kernel(
    x_hbm, spacing_hbm, counts_hbm, first_hbm, last_hbm, direction_hbm, target_hbm,
    w1_hbm, w2_hbm, w3_hbm, head_hbm,
    seg_ref, x_ref, h1_ref, h2_ref, save_ref, w16_ref, w2_ref, target_ref,
    w1_ref, w3_ref, head_ref, spacing_ref, counts_ref, first_ref, last_ref, direction_ref, out8, sems, *, n_bits,
):
    samples, _, rays = out8.shape
    count = x_ref.shape[0]
    first_rows = min(FIRST_LOAD, samples) * rays
    moves = [
        pltpu.make_async_copy(source, place, sems.at[i])
        for i, (source, place) in enumerate(
            (
                (head_hbm, head_ref), (w3_hbm, w3_ref), (w1_hbm, w1_ref), (w2_hbm, w2_ref),
                (spacing_hbm, spacing_ref), (counts_hbm, counts_ref), (first_hbm, first_ref),
                (last_hbm, last_ref), (direction_hbm, direction_ref), (target_hbm, target_ref),
            )
        )
    ]
    loads = [
        pltpu.make_async_copy(x_hbm.at[pl.ds(at, size)], x_ref.at[pl.ds(at, size)], sems.at[len(moves) + i])
        for i, (at, size) in enumerate(((0, first_rows), (first_rows, count - first_rows)))
    ]
    for move in moves[2:3] + loads[:1] + moves[3:4] + moves[:2] + loads[1:] + moves[4:]:
        move.start()
    for move in moves[:4] + loads[:1]:
        move.wait()
    w16_ref[...] = projection(head_ref[...], w3_ref[...])

    for c in range(samples + 2):
        if c == first_rows // rays:
            for move in moves[4:] + loads[1:]:
                move.wait()
        if c < samples:
            rows = pl.ds(c * rays, rays)
            h1_ref[rows] = positive(dot_nn(x_ref[rows], w1_ref[...]))
        if 0 <= c - 1 < samples:
            rows = pl.ds((c - 1) * rays, rays)
            h2_ref[rows] = positive(dot_nn(h1_ref[rows], w2_ref[...]))
        if 0 <= c - 2 < samples:
            out8[c - 2] = dot_nt(w16_ref[...], h2_ref[pl.ds((c - 2) * rays, rays)])[:8]

    slab = lax.axis_index("slab")
    reverse = jnp.minimum(jnp.maximum(direction_ref[...], 0), 1)
    ahead = [(1 - (reverse ^ ((slab >> bit) & 1))).astype(F32) for bit in range(n_bits)]
    ahead += [jnp.zeros_like(ahead[0])] * (seg_ref.shape[0] - 4 - n_bits)
    density = out8[:, 0, :]
    proj = [out8[:, 1 + k, :] + out8[:, 4 + k, :] for k in range(3)]
    ids = lax.broadcasted_iota(jnp.int32, density.shape, 0)
    active = (first_ref[...] <= slab) & (slab < last_ref[...])
    live = jnp.where((ids < counts_ref[...]) & active, 1.0, 0.0)
    span = spacing_ref[...] * live
    optical = (jnp.maximum(density, 0.0) + jnp.log1p(jnp.exp(-jnp.abs(density)))) * span
    running = running_sum(optical)
    column = running[samples - 1 : samples]
    before = jnp.where(direction_ref[...] > 0, column - running, running - optical)
    reach = jnp.exp(-before)
    passed = jnp.exp(-optical)
    weights = reach * (1.0 - passed)
    seg_ref[...] = jnp.concatenate(
        [jnp.exp(-column)] + [jnp.sum(weights * p, axis=0, keepdims=True) for p in proj] + ahead, axis=0
    )
    save_ref[0] = weights
    save_ref[1] = reach * passed
    save_ref[2] = span * jax.nn.sigmoid(density)
    for k in range(3):
        save_ref[3 + k] = proj[k]


def backward_kernel(
    own_ref, h1_ref, h2_ref, save_ref, w16_ref, w2_ref, target_ref, *refs, n_bits, n_tile,
):
    pieces = refs[:n_bits]
    front_hbm, keep_ref, send_ref, one_ref, q16, front_ref, q8, mid_ref, sem = refs[n_bits:]
    samples, _, rays = q8.shape
    count = h1_ref.shape[0]
    slab = lax.axis_index("slab")
    kept = kept_half(lax.axis_index("tile"), n_tile)

    front_trans = back_trans = jnp.ones((1, rays), F32)
    front_color = back_color = jnp.zeros((3, rays), F32)
    for bit in range(n_bits):
        behind = own_ref[4 + bit : 5 + bit] > 0
        trans, color = pieces[bit][1, 0:1], pieces[bit][1, 1:4]
        front_color = jnp.where(behind, front_color, color + trans * front_color)
        front_trans = jnp.where(behind, front_trans, trans * front_trans)
        back_color = jnp.where(behind, back_color + back_trans * color, back_color)
        back_trans = jnp.where(behind, back_trans * trans, back_trans)
    forward_ray = own_ref[4:5] + (slab & 1).astype(F32) == 1.0
    front_ref[...] = front_trans
    store = pltpu.make_async_copy(front_ref, front_hbm, sem)
    store.start()
    own = own_ref[...]
    own_trans = own[0:1]
    logits = front_color + front_trans * own[1:4] + (front_trans * own_trans) * back_color
    shade = jax.nn.sigmoid(logits)
    error = (shade - target_ref[...]) / rays
    grad_logit = error * shade * (1.0 - shade)
    grad_trans = front_trans * jnp.sum(grad_logit * back_color, axis=0, keepdims=True)
    pull = front_trans * grad_logit

    weights = save_ref[0]
    grad_weight = pull[0:1] * save_ref[3] + pull[1:2] * save_ref[4] + pull[2:3] * save_ref[5]
    product = weights * grad_weight
    running = running_sum(product)
    total = running[samples - 1 : samples]
    after = jnp.where(forward_ray, total - running, running - product)
    grad_optical = grad_weight * save_ref[1] - after - grad_trans * own_trans
    q8[:, 0, :] = grad_optical * save_ref[2]
    for k in range(3):
        q = weights * pull[k : k + 1]
        q8[:, 1 + k, :] = q
        q8[:, 4 + k, :] = q
    q8[:, 7, :] = jnp.zeros_like(weights)
    for j in range(samples):
        rows = q8[j]
        high = rows.astype(BF16).astype(F32)
        q16[:, j * rays : (j + 1) * rays] = jnp.concatenate([high, rows - high], axis=0).astype(BF16)

    chunk = count // BACKWARD_CHUNKS
    def back_two(c):
        rows = pl.ds(c * chunk, chunk)
        return where_positive(h2_ref[rows], dot_tn(q16[:, rows], w16_ref[...]))

    later = back_two(0)
    for c in range(BACKWARD_CHUNKS):
        rows = pl.ds(c * chunk, chunk)
        now = later
        if c + 1 < BACKWARD_CHUNKS:
            later = back_two(c + 1)
        grad_mid = dot_tn(h1_ref[rows], now)
        mid_ref[...] = grad_mid if c == 0 else mid_ref[...] + grad_mid
        one_ref[rows] = where_positive(h1_ref[rows], dot_nt(now, w2_ref[...]))

    half = mid_ref.shape[0] // 2
    for place, which in ((send_ref, 1 - kept), (keep_ref, kept)):
        place[...] = mid_ref[pl.ds(pl.multiple_of(which * half, half), half)]
    store.wait()


def first_kernel(x_ref, one_ref, h2_ref, q16, keep_ref, send_ref, in_ref, out_ref, *, n_tile):
    kept = kept_half(lax.axis_index("tile"), n_tile)
    count = x_ref.shape[0]
    chunk = count // FIRST_CHUNKS
    for c in range(FIRST_CHUNKS):
        rows = pl.ds(c * chunk, chunk)
        grad_in = dot_tn(x_ref[rows], one_ref[rows])
        grad_out = dot_nn(q16[:, rows], h2_ref[rows])
        for ref, part in ((out_ref, grad_out), (in_ref, grad_in)):
            ref[...] = part if c == 0 else ref[...] + part

    half = in_ref.shape[0] // 2
    for place, which in ((send_ref, 1 - kept), (keep_ref, kept)):
        rows = pl.ds(pl.multiple_of(which * half, half), half)
        lanes = place.shape[1]
        place[:half] = in_ref[rows, :lanes]
        place[half : 2 * half] = in_ref[rows, lanes:]
        four = out_ref[:4] + out_ref[8:12]
        place[2 * half :] = jnp.concatenate([four[:, :lanes], four[:, lanes:]], axis=0)


def expand_kernel(factors_ref, head_ref, out_ref):
    packed = factors_ref[factors_ref.shape[0] - 8 :]
    factors = jnp.concatenate([packed[:4], packed[4:]], axis=1)
    factors = jnp.concatenate([factors, jnp.zeros_like(factors)], axis=0)
    head = head_ref[...]
    width = head.shape[1]
    first = jnp.where(lax.broadcasted_iota(jnp.int32, (1, width), 1) == 0, 1.0, 0.0)
    rows = jnp.concatenate([first, head, jnp.zeros((4, width), F32)], axis=0)
    out_ref[...] = lax.dot_general(
        rows, factors, (((0,), (0,)), ((), ())), preferred_element_type=F32, precision=lax.Precision.HIGHEST
    )


def final_kernel(own_mid, other_mid, own_in, other_in, out_ref, in_hbm, mid_hbm, out_hbm, sems, *, n_tile):
    kept = kept_half(lax.axis_index("tile"), n_tile)
    half_mid = mid_hbm.shape[0] // 2
    half_in = in_hbm.shape[0] // 2
    lanes = own_in.shape[1]
    moves = []
    for source, place, start, size, half, columns in (
        (own_mid, mid_hbm, 0, half_mid, kept, pl.ds(0, 2 * lanes)),
        (other_mid, mid_hbm, 0, half_mid, 1 - kept, pl.ds(0, 2 * lanes)),
        (own_in, in_hbm, 0, half_in, kept, pl.ds(0, lanes)),
        (own_in, in_hbm, half_in, half_in, kept, pl.ds(lanes, lanes)),
        (other_in, in_hbm, 0, half_in, 1 - kept, pl.ds(0, lanes)),
        (other_in, in_hbm, half_in, half_in, 1 - kept, pl.ds(lanes, lanes)),
    ):
        moves.append(
            pltpu.make_async_copy(
                source.at[pl.ds(start, size)],
                place.at[pl.ds(pl.multiple_of(half * size, size), size), columns],
                sems.at[len(moves)],
            )
        )
    moves.append(pltpu.make_async_copy(out_ref, out_hbm, sems.at[len(moves)]))
    for move in moves:
        move.start()
    for move in moves:
        move.wait()


def kept_half(tile, n_tile):
    half = tile & 1
    shift = 1
    while (1 << shift) < n_tile:
        half = half ^ ((tile >> shift) & 1)
        shift += 1
    return half


def joined(own, got, own_first):
    first = jnp.where(own_first, own, got)
    second = jnp.where(own_first, got, own)
    row = lax.broadcasted_iota(jnp.int32, own.shape, 1)
    return first[:, 0:1] * second + jnp.where(row == 0, 0.0, first)


def pairs(size, bit):
    return [(i, i ^ bit) for i in range(size)]


def make_body(n_slab, n_tile):

    def body(
        encoded, spacing, counts, seg_first, seg_last, direction,
        field_in, field_mid, field_out, color_head, target,
    ):
        _, samples, rays, width = encoded.shape
        hidden = field_mid.shape[1]
        features = field_out.shape[2]
        count = samples * rays
        n_bits = (n_slab - 1).bit_length()
        row = lambda a: a.reshape(1, rays)
        seg_rows = 8 * ((4 + n_bits + 7) // 8)
        seg, *kept = pl.pallas_call(
            functools.partial(forward_kernel, n_bits=n_bits),
            name="forward",
            out_shape=(
                pltpu.VMEM((seg_rows, rays), F32),
                pltpu.VMEM((count, width), BF16),
                pltpu.VMEM((count, hidden), BF16),
                pltpu.VMEM((count, hidden), BF16),
                pltpu.VMEM((6, samples, rays), F32),
                pltpu.VMEM((16, hidden), BF16),
                pltpu.VMEM((hidden, hidden), BF16),
                pltpu.VMEM((3, rays), F32),
            ),
            in_specs=[HBM] * 11,
            out_specs=(VMEM,) * 8,
            scratch_shapes=[
                pltpu.VMEM((width, hidden), BF16),
                pltpu.VMEM((features, hidden), BF16),
                pltpu.VMEM((3, features), F32),
                pltpu.VMEM((samples, rays), F32),
                pltpu.VMEM((1, rays), jnp.int32),
                pltpu.VMEM((1, rays), jnp.int32),
                pltpu.VMEM((1, rays), jnp.int32),
                pltpu.VMEM((1, rays), jnp.int32),
                pltpu.VMEM((samples, 8, rays), F32),
                pltpu.SemaphoreType.DMA((12,)),
            ],
            compiler_params=LIMIT,
        )(
            *(
                pltpu.with_memory_space_constraint(a, pltpu.HBM)
                for a in (
                    encoded[0].reshape(count, width), spacing[0], counts, row(seg_first), row(seg_last),
                    row(direction), target.T, field_in[0], field_mid[0], field_out[0].T, color_head.T,
                )
            ),
        )

        both = jnp.stack([seg, lax.ppermute(seg, "tile", pairs(n_tile, 1))])
        block = both[:, :4]
        pieces = []
        for bit in range(n_bits):
            got = lax.ppermute(block, ("slab", "tile"), pairs(n_slab * n_tile, (n_tile << bit) | 1))
            pieces.append(got)
            if bit + 1 < n_bits:
                block = joined(block, got[::-1], both[:, 4 + bit : 5 + bit] > 0)

        x, h1, h2, save, w16, w2, target_rows = kept
        half_mid, half_in = hidden // 2, width + 8
        front, keep_mid, send_mid, back_one, factors = pl.pallas_call(
            functools.partial(backward_kernel, n_bits=n_bits, n_tile=n_tile),
            name="backward",
            out_shape=(
                pltpu.HBM((1, rays), F32),
                pltpu.VMEM((half_mid, hidden), F32),
                pltpu.VMEM((half_mid, hidden), F32),
                pltpu.VMEM((count, hidden), BF16),
                pltpu.VMEM((16, count), BF16),
            ),
            in_specs=[VMEM] * (7 + n_bits),
            out_specs=(HBM, VMEM, VMEM, VMEM, VMEM),
            scratch_shapes=[
                pltpu.VMEM((1, rays), F32),
                pltpu.VMEM((samples, 8, rays), F32),
                pltpu.VMEM((hidden, hidden), F32),
                pltpu.SemaphoreType.DMA,
            ],
            compiler_params=LIMIT,
            cost_estimate=pl.CostEstimate(flops=4 * count * hidden * hidden, bytes_accessed=0, transcendentals=0),
        )(seg, h1, h2, save, w16, w2, target_rows, *pieces)
        def chip_sum(keep, send):
            return keep + lax.ppermute(send, "tile", pairs(n_tile, 1))

        def tile_sum(part):
            bit = 2
            while bit < n_tile:
                part = part + lax.ppermute(part, "tile", pairs(n_tile, bit | 1))
                bit *= 2
            return part, lax.ppermute(part, "tile", pairs(n_tile, 1))

        part_mid = chip_sum(keep_mid, send_mid)
        keep_in, send_in = pl.pallas_call(
            functools.partial(first_kernel, n_tile=n_tile),
            name="first",
            out_shape=(pltpu.VMEM((half_in, hidden // 2), F32), pltpu.VMEM((half_in, hidden // 2), F32)),
            in_specs=[VMEM] * 4,
            out_specs=(VMEM, VMEM),
            scratch_shapes=[pltpu.VMEM((width, hidden), F32), pltpu.VMEM((16, hidden), F32)],
            compiler_params=LIMIT,
            cost_estimate=pl.CostEstimate(flops=4 * count * hidden * hidden, bytes_accessed=0, transcendentals=0),
        )(x, back_one, h2, factors)

        part_mid, keep_in, send_in = lax.optimization_barrier((part_mid, keep_in, send_in))
        own_mid, other_mid = tile_sum(part_mid)
        own_in, other_in = tile_sum(chip_sum(keep_in, send_in))
        expanded = pl.pallas_call(
            expand_kernel,
            name="expand",
            out_shape=pltpu.VMEM((features, hidden), F32),
            in_specs=[VMEM] * 2,
            out_specs=VMEM,
            compiler_params=LIMIT,
            cost_estimate=pl.CostEstimate(flops=2 * 8 * features * hidden * 6, bytes_accessed=0, transcendentals=0),
        )(own_in, color_head.T)
        grad_in, grad_mid, grad_out = pl.pallas_call(
            functools.partial(final_kernel, n_tile=n_tile),
            name="final",
            out_shape=(
                pltpu.HBM((width, hidden), F32),
                pltpu.HBM((hidden, hidden), F32),
                pltpu.HBM((features, hidden), F32),
            ),
            in_specs=[VMEM] * 5,
            out_specs=(HBM,) * 3,
            scratch_shapes=[pltpu.SemaphoreType.DMA((7,))],
            compiler_params=LIMIT,
        )(own_mid, other_mid, own_in, other_in, expanded)
        return front, grad_in[None], grad_mid[None], grad_out.T[None]

    return body


def solution(mesh):
    return jax.shard_map(
        make_body(mesh.shape["slab"], mesh.shape["tile"]),
        mesh=mesh,
        in_specs=(
            P("slab", None, "tile", None),
            P("slab", None, "tile"),
            P("slab", "tile"),
            P("tile"),
            P("tile"),
            P("tile"),
            P("slab", None, None),
            P("slab", None, None),
            P("slab", None, None),
            P(),
            P("tile", None),
        ),
        out_specs=(
            P("slab", "tile"),
            P("slab", None, None),
            P("slab", None, None),
            P("slab", None, None),
        ),
        check_vma=False,
    )
```
